1024 devices in a mesh: expert: 64 (over x, y), head: 16 (over z, core).
Axes of the slice: x: 8, y: 8, z: 8, core: 2. Of those that a mesh axis runs over, the one named last changes fastest.
Arguments:
- latent: bfloat16 [2048, 1024], P('expert'), may hold values from -6 to 6
- routes: int32 [2048, 22], P('expert'), may hold values from 0 to 255, all different within a row; in each aligned block of 32 rows (0 to 31, 32 to 63, ...) at most 4 rows name the same one
- gate_q: int32 [2048, 22], P('expert'), may hold values from 1 to 255
- up_weight: bfloat16 [256, 1024, 2048], P('expert', None, 'head'), may hold values from -0.1875 to 0.1875
- down_weight: bfloat16 [256, 2048, 1024], P('expert', 'head'), may hold values from -0.125 to 0.125
- out_weight: bfloat16 [1024, 4096], P(None, 'head'), may hold values from -0.1875 to 0.1875
- cotangent: bfloat16 [2048, 4096], P('expert', 'head'), may hold values from -6 to 6
Outputs:
- mixed: bfloat16 [2048, 4096], P('expert', 'head')
- grad_up: bfloat16 [256, 1024, 2048], P('expert', None, 'head')
The draws below stay inside these ranges and needn't reach their ends.
Inputs may be any that keep to these rules, and one draw needn't show every extreme that they name: `routes`: each row names 22 different experts. In each aligned block of 32 rows (the tokens of one index of expert) no expert is named by more than 4 rows, a bound that some block reaches.
All inputs are finite; a program needn't handle non-finite values.
Results may differ from the reference program's by a relative error of at most 0.029.
Values may be sent and summed in bfloat16 or wider, within the bound.
No kernel may reach another device: no remote copies, remote signals or barrier semaphores. Data moves between devices by JAX's collectives and lax.ppermute only.
A program may use at most 64 MiB of HBM per device.

```python
import math
import jax
import jax.numpy as jnp
import numpy as np
from jax import lax

D = 4096
L = 1024
EH = 2048
TOP = 22
TOK_GRP = 32
EXPERTS = 256
TOKENS = 2048
MOST = 4
N_EXPERT = 64
N_HEAD = 16


def touch_ends(array, rng, least, top_value):
    index_at = [jax.random.randint(jax.random.fold_in(rng, axis), (), 0, length) for axis, length in enumerate(array.shape)]
    main_axis = array.shape.index(max(array.shape))
    beside = index_at[:main_axis] + [(index_at[main_axis] + 1) % array.shape[main_axis]] + index_at[main_axis + 1:]
    return array.at[tuple(index_at)].set(least).at[tuple(beside)].set(top_value)


def block_levels(rng, extent, split, least, high):
    loudness, own = 1.0, jax.random.fold_in(rng, 6)
    for axis_at, blocks in split:
        heights = jnp.exp(jax.random.uniform(jax.random.fold_in(own, axis_at), (blocks,), jnp.float32, least / len(split), high / len(split)))
        loudness = loudness * jnp.repeat(heights, extent[axis_at] // blocks).reshape([-1 if axis == axis_at else 1 for axis in range(len(extent))])
    return loudness


def deal_out(own_key, own, number, rows, amount, top, most, lean):
    sequence = jax.random.permutation(own_key, amount)
    crowded, usual = shares(amount, rows * top, most, lean, True), shares(amount, rows * top, most, lean, False)
    places = jnp.arange(amount)

    def named(tallies, turn):
        used = int((tallies > 0).sum())
        fixed = max(1, used // 4)
        passed = fixed + (places - fixed + turn * (used - fixed)) % max(1, amount - fixed)
        return jnp.zeros((amount,), jnp.int32).at[sequence[jnp.where(places < fixed, places, passed)]].set(jnp.asarray(tallies, jnp.int32))

    tallies = jnp.where(number % 4 == 0, named(crowded, number // 4), named(usual, number - number // 4 - 1))
    mixed = jax.random.permutation(jax.random.fold_in(own, 3), amount)
    donor, taker = mixed[0:amount // 2 * 2:2], mixed[1:amount // 2 * 2:2]
    margin = jnp.minimum(tallies[donor] - 1, most - tallies[taker]) // 2
    margin = jnp.where((donor == sequence[0]) | (taker == sequence[0]) | (tallies[taker] == 0), 0, jnp.maximum(margin, 0))
    passed = jax.random.randint(jax.random.fold_in(own, 4), (amount // 2,), 0, 1 << 20) % (margin + 1)
    tallies = tallies.at[donor].add(-passed).at[taker].add(passed)
    members = jnp.searchsorted(jnp.cumsum(tallies), jnp.arange(rows * top), side="right").astype(jnp.int32)
    table = members.reshape(top, rows).T
    table = table[jax.random.permutation(jax.random.fold_in(own, 1), rows)]
    turn = jax.random.randint(jax.random.fold_in(own, 2), (rows, 1), 0, top)
    return jnp.take_along_axis(table, (jnp.arange(top)[None, :] + turn) % top, axis=1)


def shares(count, total, most, skew, full):
    portions = [(1 << 20) // math.isqrt(standing ** skew) + 1 for standing in range(1, count + 1)]
    largest = most if full else min(most, max(-(-total // count), total * portions[0] // sum(portions)))
    least = 1 if total - largest >= count - 1 else 0
    counts, rest = [largest] + [least] * (count - 1), total - largest - least * (count - 1)
    while rest > 0:
        movable = [i for i in range(1, count) if counts[i] < largest] or [i for i in range(1, count) if counts[i] < most]
        whole, remaining = sum([portions[i] for i in movable]), rest
        for i in movable:
            more = min(most - counts[i], max(1, remaining * portions[i] // whole), rest)
            counts[i] = counts[i] + more
            rest = rest - more
    return np.array(counts)


def scatter_about(rng, extent, scale, bound, split=(), kind=jnp.bfloat16):
    level = block_levels(rng, extent, split, -0.22, 0.18) if split else 1.0
    result = jax.random.normal(rng, extent, jnp.float32) * scale * level
    return jnp.minimum(jnp.maximum(result, -bound), bound).astype(kind)


def setup_inputs(seed: int = 0) -> dict:
    key_list = jax.random.split(jax.random.key(seed), 8)
    latent = scatter_about(key_list[0], (TOKENS, L), 1.0, 6.0, ((0, 64),))
    routes_keys = jax.random.split(jax.random.fold_in(key_list[1], 1), TOKENS // TOK_GRP)
    routes_turns = jax.random.permutation(jax.random.fold_in(key_list[1], 3), TOKENS // TOK_GRP)
    routes = jax.vmap(lambda own, number: deal_out(jax.random.fold_in(key_list[1], 2), own, number, TOK_GRP, EXPERTS, TOP, MOST, 2))(routes_keys, routes_turns).reshape((TOKENS, TOP))
    gate_q = touch_ends(jax.random.randint(key_list[2], (TOKENS, TOP), 1, 256), jax.random.fold_in(key_list[2], 1), 1, 255).astype(jnp.int32)
    up_weight = scatter_about(key_list[3], (EXPERTS, L, EH), L ** -0.5, 0.1875, ((0, 64), (2, 16)))
    down_weight = scatter_about(key_list[4], (EXPERTS, EH, L), EH ** -0.5, 0.125, ((0, 64), (1, 16)))
    out_weight = scatter_about(key_list[5], (L, D), L ** -0.5, 0.1875, ((1, 16),))
    cotangent = scatter_about(key_list[6], (TOKENS, D), 1.0, 6.0, ((0, 64), (1, 16)))
    return dict(latent=latent, routes=routes, gate_q=gate_q, up_weight=up_weight, down_weight=down_weight, out_weight=out_weight, cotangent=cotangent)


def reference(latent, routes, gate_q, up_weight, down_weight, out_weight, cotangent):
    tok_count, route_count = routes.shape
    expert_count = up_weight.shape[0]
    width = latent.shape[1]
    head_width = up_weight.shape[2] // N_HEAD
    capacity = N_EXPERT * MOST
    total_routes = tok_count * route_count
    gates = gate_q.astype(jnp.float32)
    gates = gates / jnp.sum(gates, axis=1, keepdims=True)
    flat_gates = gates.reshape(-1)
    flat_ids = routes.reshape(-1).astype(jnp.int32)
    ordering = jnp.argsort(flat_ids, stable=True).astype(jnp.int32)
    sorted_ids = flat_ids[ordering]
    experts_iota = jnp.arange(expert_count, dtype=jnp.int32)
    starts = jnp.searchsorted(sorted_ids, experts_iota, side="left").astype(jnp.int32)
    ends_at = jnp.searchsorted(sorted_ids, experts_iota, side="right").astype(jnp.int32)
    back = jnp.dot(cotangent, out_weight.T, preferred_element_type=jnp.float32)

    def per_expert(expert):
        indices = starts[expert] + jnp.arange(capacity, dtype=jnp.int32)
        in_use = indices < ends_at[expert]
        chosen = ordering[jnp.minimum(indices, total_routes - 1)]
        tok_index = (chosen // route_count).astype(jnp.int32)
        gathered = jnp.where(in_use[:, None], latent[tok_index], jnp.zeros((), jnp.bfloat16))
        gate_rows = jnp.where(in_use, flat_gates[chosen], jnp.float32(0.0))
        w_up = up_weight[expert]
        w_down = down_weight[expert]
        pre_act = jnp.dot(gathered, w_up, preferred_element_type=jnp.float32)
        hidden = (jnp.maximum(pre_act, 0.0) ** 2).astype(jnp.bfloat16)
        portion = jnp.einsum("chf,hfl->chl",
                             hidden.reshape(capacity, N_HEAD, head_width).astype(jnp.float32),
                             w_down.reshape(N_HEAD, head_width, width).astype(jnp.float32)).astype(jnp.bfloat16)
        contrib = gate_rows[:, None] * jnp.sum(portion.astype(jnp.float32), axis=1)
        grad_rows = (gate_rows[:, None] * back[tok_index]).astype(jnp.bfloat16)
        hidden_grad = jnp.dot(grad_rows, w_down.T, preferred_element_type=jnp.float32)
        pre_grad = (hidden_grad * 2.0 * jnp.maximum(pre_act, 0.0)).astype(jnp.bfloat16)
        grad_one = jnp.dot(gathered.T, pre_grad, preferred_element_type=jnp.float32).astype(jnp.bfloat16)
        return contrib, tok_index, grad_one

    contribs, tok_indices, grad_up = lax.map(per_expert, experts_iota)
    combined = jnp.zeros((tok_count, width), jnp.float32)
    combined = combined.at[tok_indices.reshape(-1)].add(contribs.reshape(-1, width))
    mixed = jnp.dot(combined.astype(jnp.bfloat16), out_weight, preferred_element_type=jnp.float32).astype(jnp.bfloat16)
    return mixed, grad_up
```

```python
import functools

import jax
import jax.numpy as jnp
from jax import lax
from jax.experimental import pallas as pl
from jax.experimental.pallas import tpu as pltpu
from jax.sharding import PartitionSpec as P

F32 = jnp.float32
BF16 = jnp.bfloat16
QUAD = 4
MOST = 4
ROWS = 2 * MOST
VMEM = pl.BlockSpec(memory_space=pltpu.VMEM)
SMEM = pl.BlockSpec(memory_space=pltpu.SMEM)


def call(kernel, outs, *args, scalars=0, flops=0):
    single = not isinstance(outs, (list, tuple))
    moved = sum(a.size * a.dtype.itemsize for a in args)
    return pl.pallas_call(
        kernel,
        out_shape=outs,
        in_specs=[SMEM] * scalars + [VMEM] * (len(args) - scalars),
        out_specs=VMEM if single else [VMEM] * len(outs),
        compiler_params=pltpu.CompilerParams(vmem_limit_bytes=40 * 2**20),
        cost_estimate=pl.CostEstimate(flops=flops, bytes_accessed=2 * moved, transcendentals=0),
    )(*args)


def shape(*dims, dtype=BF16):
    return jax.ShapeDtypeStruct(dims, dtype)


def dot(a, b, dims, precision=None):
    return lax.dot_general(a, b, (dims, ((), ())), precision=precision, preferred_element_type=F32)


def to_blocks(rows):
    parts = []
    for a in range(rows.shape[0] // 8):
        for b in range(rows.shape[1] // 256):
            parts.append(rows[8 * a : 8 * a + 8, 256 * b : 256 * b + 256])
    return jnp.concatenate(parts, axis=0)


def from_blocks(blocks, columns):
    per_row = columns // 256
    strips = []
    for a in range(blocks.shape[0] // (8 * per_row)):
        at = 8 * per_row * a
        strips.append(
            jnp.concatenate([blocks[at + 8 * b : at + 8 * b + 8] for b in range(per_row)], axis=1)
        )
    return jnp.concatenate(strips, axis=0)


def back_kernel(cot_ref, out_w_ref, o_ref):
    part = dot(cot_ref[...], out_w_ref[...], ((1,), (1,)))
    o_ref[...] = to_blocks(part).astype(BF16)


def sum_kernel(i_ref, o_ref):
    blocks = i_ref[...].astype(F32)
    total = blocks[0:8]
    for p in range(1, blocks.shape[0] // 8):
        total = total + blocks[8 * p : 8 * p + 8]
    o_ref[...] = jnp.concatenate([total] * (blocks.shape[0] // 8), axis=0).astype(BF16)


def send_kernel(me_ref, table_ref, latent_ref, back_ref, send_ref, coef_ref):
    count = send_ref.shape[0]
    tokens = latent_ref.shape[0]
    top = table_ref.shape[0] // 2
    row = lax.broadcasted_iota(jnp.int32, (count, tokens), 0)
    expert = QUAD * (row // ROWS) + me_ref[0]
    score = jnp.zeros((count, tokens), jnp.int32)
    total = jnp.zeros((1, tokens), jnp.int32)
    for k in range(top):
        q = table_ref[top + k : top + k + 1, :]
        total = total + q
        score = score + jnp.where(table_ref[k : k + 1, :] == expert, q, 0)
    score = score.astype(F32)
    named = score > 0.0
    earlier = lax.broadcasted_iota(jnp.int32, (tokens, tokens), 0)
    later = lax.broadcasted_iota(jnp.int32, (tokens, tokens), 1)
    before = jnp.where(earlier < later, 1.0, 0.0).astype(BF16)
    rank = dot(jnp.where(named, 1.0, 0.0).astype(BF16), before, ((1,), (0,)))
    here = named & (rank == (row % MOST).astype(F32))
    coef_ref[...] = jnp.where(here, score, 0.0).astype(BF16)
    pick = jnp.where(here, 1.0, 0.0).astype(BF16)
    gate = jnp.sum(jnp.where(here, score / total.astype(F32), 0.0), axis=1, keepdims=True)
    latent_rows = dot(pick, latent_ref[...], ((1,), (0,)))
    back = from_blocks(back_ref[...].astype(F32), latent_ref.shape[1]).astype(BF16)
    back_rows = dot(pick, back, ((1,), (0,)))
    is_latent = lax.broadcasted_iota(jnp.int32, (count, 1), 0) % ROWS < MOST
    send_ref[...] = jnp.where(is_latent, latent_rows, gate * back_rows).astype(BF16)


def pack_kernel(me_ref, up_ref, down_ref, *outs):
    width, unit = up_ref.shape[1], up_ref.shape[2]
    for d, o_ref in enumerate(outs, 1):
        expert = me_ref[0] ^ d
        o_ref[0:width, :] = up_ref[expert]
        for b in range(width // unit):
            o_ref[width + unit * b : width + unit * (b + 1), :] = down_ref[
                expert, :, unit * b : unit * (b + 1)
            ]


def expert_kernel(me_ref, rows_ref, up_ref, down_ref, *refs):
    packs, (out_ref, *grad_refs) = refs[: QUAD - 1], refs[QUAD - 1 :]
    width, unit = up_ref.shape[1], up_ref.shape[2]
    count = rows_ref.shape[0]
    half = width // 2
    me = me_ref[0]
    blocks = width // unit
    ups = [up_ref[me]] + [p[0:width, :] for p in packs]
    downs = [down_ref[me]] + [
        jnp.concatenate(
            [p[width + unit * b : width + unit * (b + 1), :] for b in range(blocks)], axis=1
        )
        for p in packs
    ]
    up = jnp.concatenate(ups, axis=1)
    down = jnp.concatenate(downs, axis=0)
    rows = rows_ref[...]
    is_latent = lax.broadcasted_iota(jnp.int32, (count, 1), 0) % ROWS < MOST
    act = jnp.maximum(dot(rows, up, ((1,), (0,))), 0.0)
    hidden = act * act
    hidden = jnp.where(is_latent, hidden, pltpu.roll(hidden, MOST, 0)).astype(BF16)
    left = dot(hidden, down[:, :half], ((1,), (0,)))
    right = dot(hidden, down[:, half:], ((1,), (0,)))
    out_ref[...] = jnp.where(is_latent, left, right).astype(BF16)
    hidden_grad = pltpu.roll(dot(rows, down, ((1,), (1,))), count - MOST, 0)
    pre_grad = jnp.where(is_latent, hidden_grad * 2.0 * act, 0.0).astype(BF16)
    grad = dot(rows, pre_grad, ((0,), (0,))).astype(BF16)
    for d, g_ref in enumerate(grad_refs):
        g_ref[...] = grad[:, unit * d : unit * (d + 1)]


def combine_kernel(rows_ref, coef_ref, gate_ref, o_ref):
    count = rows_ref.shape[0]
    is_left = lax.broadcasted_iota(jnp.int32, (count, 1), 0) % ROWS < MOST
    coef = coef_ref[...].astype(F32)
    left = jnp.where(is_left, coef, 0.0).astype(BF16)
    right = jnp.where(is_left, 0.0, coef).astype(BF16)
    rows = rows_ref[...]
    total = jnp.sum(gate_ref[...].astype(F32), axis=1, keepdims=True)
    parts = [dot(c, rows, ((0,), (0,))) / total for c in (left, right)]
    o_ref[...] = to_blocks(jnp.concatenate(parts, axis=1)).astype(BF16)


def mixed_kernel(blocks_ref, out_w_ref, o_ref):
    combined = from_blocks(blocks_ref[...].astype(F32), out_w_ref.shape[0]).astype(BF16)
    o_ref[...] = dot(combined, out_w_ref[...], ((1,), (0,))).astype(BF16)


def grad_kernel(me_ref, *refs):
    grads, o_ref = refs[:-1], refs[-1]
    for d, g_ref in enumerate(grads):
        o_ref[me_ref[0] ^ d] = g_ref[...]


def exchange(rows, axis):
    peers = lax.axis_size(axis)
    split = rows.reshape(peers, rows.shape[0] // peers, rows.shape[1])
    moved = lax.all_to_all(split, axis, split_axis=0, concat_axis=0, tiled=True)
    return moved.reshape(rows.shape)


def sum_over_head(blocks):
    return exchange(call(sum_kernel, shape(*blocks.shape), exchange(blocks, "head")), "head")


def swap(array, distance):
    members = lax.axis_size("head")
    return lax.ppermute(array, "head", [(i, i ^ distance) for i in range(members)])


def per_device(latent, routes, gate_q, up_weight, down_weight, out_weight, cotangent):
    groups = lax.axis_size("expert")
    tokens, width = latent.shape
    unit = up_weight.shape[2]
    count = groups * ROWS
    me = (lax.axis_index("head") % QUAD).astype(jnp.int32).reshape(1)
    table = jnp.concatenate([routes, gate_q], axis=1).T

    packs = call(
        pack_kernel,
        [shape(2 * width, unit)] * (QUAD - 1),
        me, up_weight, down_weight, scalars=1,
    )
    packs = [swap(p, d) for d, p in enumerate(packs, 1)]

    back = call(
        back_kernel, shape(tokens * width // 256, 256), cotangent, out_weight,
        flops=2 * tokens * width * cotangent.shape[1],
    )
    back = sum_over_head(back)
    send, coef = call(
        send_kernel, [shape(count, width), shape(count, tokens)], me, table, latent, back, scalars=1
    )
    rows = exchange(send, "expert")
    out, *grads = call(
        expert_kernel,
        [shape(count, width // 2)] + [shape(width, unit)] * QUAD,
        me, rows, up_weight, down_weight, *packs,
        scalars=1, flops=8 * count * width * unit * QUAD,
    )
    grads = [grads[0]] + [swap(g, d) for d, g in enumerate(grads[1:], 1)]
    returned = exchange(out, "expert")
    comb = call(combine_kernel, shape(tokens * width // 256, 256), returned, coef, gate_q)
    comb = sum_over_head(comb)
    mixed = call(
        mixed_kernel, shape(tokens, out_weight.shape[1]), comb, out_weight,
        flops=2 * tokens * width * out_weight.shape[1],
    )
    grad_up = call(grad_kernel, shape(*up_weight.shape), me, *grads, scalars=1)
    return (mixed, grad_up)


def solution(mesh):
    placed = (
        P("expert", None),
        P("expert", None),
        P("expert", None),
        P("expert", None, "head"),
        P("expert", "head", None),
        P(None, "head"),
        P("expert", "head"),
    )
    return jax.shard_map(
        per_device,
        mesh=mesh,
        in_specs=placed,
        out_specs=(P("expert", "head"), P("expert", None, "head")),
        check_vma=False,
    )
```

```python
import jax
import jax.numpy as jnp
from jax import lax
from jax.experimental import pallas as pl
from jax.experimental.pallas import tpu as pltpu
from jax.sharding import Mesh, PartitionSpec as P

F32 = jnp.float32
BF16 = jnp.bfloat16
HEAD = ("z", "core")
QUAD = 4
CHUNKS = 4
MOST = 4
ROWS = 2 * MOST
ANY = pl.BlockSpec(memory_space=pl.ANY)
VMEM = pl.BlockSpec(memory_space=pltpu.VMEM)
SMEM = pl.BlockSpec(memory_space=pltpu.SMEM)


def call(kernel, outs, *args, scalars=0, flops=0, in_hbm=(), out_hbm=(), scratch=()):
    single = not isinstance(outs, (list, tuple))
    moved = sum(a.size * a.dtype.itemsize for a in args)
    ins = [SMEM if i < scalars else ANY if i in in_hbm else VMEM for i in range(len(args))]
    places = [ANY if i in out_hbm else VMEM for i in range(1 if single else len(outs))]
    return pl.pallas_call(
        kernel,
        out_shape=outs,
        in_specs=ins,
        out_specs=places[0] if single else places,
        scratch_shapes=scratch,
        compiler_params=pltpu.CompilerParams(vmem_limit_bytes=40 * 2**20),
        cost_estimate=pl.CostEstimate(flops=flops, bytes_accessed=2 * moved, transcendentals=0),
    )(*args)


def shape(*dims, dtype=BF16):
    return jax.ShapeDtypeStruct(dims, dtype)


def dot(a, b, dims, precision=None):
    return lax.dot_general(a, b, (dims, ((), ())), precision=precision, preferred_element_type=F32)


def halves(me_ref, rows):
    half = rows.shape[1] // 2
    first = me_ref[0] % 2 == 0
    left, right = rows[:, :half], rows[:, half:]
    return jnp.where(first, left, right), jnp.where(first, right, left)


def joined(me_ref, own, other):
    first = me_ref[0] % 2 == 0
    own, other = own.astype(F32), other.astype(F32)
    return jnp.concatenate([jnp.where(first, own, other), jnp.where(first, other, own)], axis=1)


def back_kernel(me_ref, cot_ref, out_w_ref, keep_ref, give_ref):
    part = dot(cot_ref[...], out_w_ref[...], ((1,), (1,)))
    keep, give = halves(me_ref, part)
    keep_ref[...] = keep
    give_ref[...] = give.astype(BF16)


def spread_kernel(keep_ref, got_ref, o_ref):
    rows = (keep_ref[...] + got_ref[...].astype(F32)).astype(BF16)
    for z in range(o_ref.shape[0]):
        o_ref[z] = rows


def sum_kernel(i_ref, o_ref):
    o_ref[...] = jnp.sum(i_ref[...].astype(F32), axis=0).astype(BF16)


def send_kernel(me_ref, table_ref, latent_ref, own_ref, other_ref, send_ref, coef_ref, buf, sems):
    count = send_ref.shape[0]
    tokens = latent_ref.shape[0]
    top = table_ref.shape[0] // 2
    step = count // CHUNKS
    back = joined(me_ref, own_ref[...], other_ref[...]).astype(BF16)
    latent = latent_ref[...]
    total = jnp.zeros((1, tokens), jnp.int32)
    for k in range(top):
        total = total + table_ref[top + k : top + k + 1, :]
    earlier = lax.broadcasted_iota(jnp.int32, (tokens, tokens), 0)
    later = lax.broadcasted_iota(jnp.int32, (tokens, tokens), 1)
    before = jnp.where(earlier < later, 1.0, 0.0).astype(BF16)
    is_latent = lax.broadcasted_iota(jnp.int32, (step, 1), 0) % ROWS < MOST
    copies = []
    for i in range(CHUNKS):
        at = pl.ds(step * i, step)
        row = lax.broadcasted_iota(jnp.int32, (step, tokens), 0) + step * i
        expert = QUAD * (row // ROWS) + me_ref[0]
        score = jnp.zeros((step, tokens), jnp.int32)
        for k in range(top):
            q = table_ref[top + k : top + k + 1, :]
            score = score + jnp.where(table_ref[k : k + 1, :] == expert, q, 0)
        score = score.astype(F32)
        named = score > 0.0
        rank = dot(jnp.where(named, 1.0, 0.0).astype(BF16), before, ((1,), (0,)))
        here = named & (rank == (row % MOST).astype(F32))
        coef_ref[at, :] = jnp.where(here, score, 0.0).astype(BF16)
        pick = jnp.where(here, 1.0, 0.0).astype(BF16)
        gate = jnp.sum(jnp.where(here, score / total.astype(F32), 0.0), axis=1, keepdims=True)
        latent_rows = dot(pick, latent, ((1,), (0,)))
        back_rows = dot(pick, back, ((1,), (0,)))
        buf[at, :] = jnp.where(is_latent, latent_rows, gate * back_rows).astype(BF16)
        copies.append(pltpu.make_async_copy(buf.at[at, :], send_ref.at[at, :], sems.at[i]))
        copies[-1].start()
    for copy in copies:
        copy.wait()


def pack_kernel(me_ref, up_ref, down_ref, *outs):
    width, unit = up_ref.shape[1], up_ref.shape[2]
    for d, o_ref in enumerate(outs, 1):
        expert = me_ref[0] ^ d
        o_ref[0:width, :] = up_ref[expert]
        for b in range(width // unit):
            o_ref[width + unit * b : width + unit * (b + 1), :] = down_ref[
                expert, :, unit * b : unit * (b + 1)
            ]


def expert_kernel(me_ref, rows_hbm, up_hbm, down_hbm, *refs):
    packs, refs = refs[: QUAD - 1], refs[QUAD - 1 :]
    out_hbm, *grads_hbm = refs[: QUAD + 1]
    rows_ref, up_ref, down_ref, out_ref, grad_ref, sems = refs[QUAD + 1 :]
    width, unit = up_hbm.shape[1], up_hbm.shape[2]
    count = rows_hbm.shape[0]
    half = width // 2
    me = me_ref[0]
    copies = []

    def fetch(source, target):
        copies.append(pltpu.make_async_copy(source, target, sems.at[len(copies)]))
        copies[-1].start()
        return copies[-1]

    first = [fetch(rows_hbm, rows_ref), fetch(up_hbm.at[me], up_ref.at[:, 0:unit])]
    for d, p in enumerate(packs, 1):
        at = pl.ds(unit * d, unit)
        first.append(fetch(p.at[pl.ds(0, width), :], up_ref.at[:, at]))
    second = [fetch(down_hbm.at[me], down_ref.at[0:unit, :])]
    for d, p in enumerate(packs, 1):
        at = pl.ds(unit * d, unit)
        for b in range(width // unit):
            block = p.at[pl.ds(width + unit * b, unit), :]
            second.append(fetch(block, down_ref.at[at, pl.ds(unit * b, unit)]))

    is_latent = lax.broadcasted_iota(jnp.int32, (count, 1), 0) % ROWS < MOST
    for copy in first:
        copy.wait()
    rows = rows_ref[...]
    act = jnp.maximum(dot(rows, up_ref[...], ((1,), (0,))), 0.0)
    hidden = act * act
    hidden = jnp.where(is_latent, hidden, pltpu.roll(hidden, MOST, 0)).astype(BF16)
    for copy in second:
        copy.wait()
    left = dot(hidden, down_ref[:, :half], ((1,), (0,)))
    right = dot(hidden, down_ref[:, half:], ((1,), (0,)))
    out_ref[...] = jnp.where(is_latent, left, right).astype(BF16)
    results = [fetch(out_ref, out_hbm)]
    hidden_grad = pltpu.roll(dot(rows, down_ref[...], ((1,), (1,))), count - MOST, 0)
    pre_grad = jnp.where(is_latent, hidden_grad * 2.0 * act, 0.0).astype(BF16)
    grad_ref[...] = dot(rows, pre_grad, ((0,), (0,))).astype(BF16)
    for d, g in enumerate(grads_hbm):
        results.append(fetch(grad_ref.at[:, pl.ds(unit * d, unit)], g))
    for copy in results:
        copy.wait()


def combine_kernel(me_ref, rows_ref, coef_ref, gate_ref, keep_ref, give_ref):
    count = rows_ref.shape[0]
    is_left = lax.broadcasted_iota(jnp.int32, (count, 1), 0) % ROWS < MOST
    coef = coef_ref[...].astype(F32)
    left = jnp.where(is_left, coef, 0.0).astype(BF16)
    right = jnp.where(is_left, 0.0, coef).astype(BF16)
    rows = rows_ref[...]
    total = jnp.sum(gate_ref[...].astype(F32), axis=1, keepdims=True)
    parts = [dot(c, rows, ((0,), (0,))) / total for c in (left, right)]
    keep, give = halves(me_ref, jnp.concatenate(parts, axis=1))
    keep_ref[...] = keep
    give_ref[...] = give.astype(BF16)


def mixed_kernel(me_ref, own_ref, other_ref, out_w_ref, o_ref):
    combined = joined(me_ref, own_ref[...], other_ref[...]).astype(BF16)
    o_ref[...] = dot(combined, out_w_ref[...], ((1,), (0,))).astype(BF16)


def grad_kernel(me_ref, *refs):
    grads, o_ref = refs[:-1], refs[-1]
    for d, g_ref in enumerate(grads):
        o_ref[me_ref[0] ^ d] = g_ref[...]


def exchange(rows, axis):
    peers = lax.axis_size(axis)
    split = rows.reshape(peers, rows.shape[0] // peers, rows.shape[1])
    moved = lax.all_to_all(split, axis, split_axis=0, concat_axis=0, tiled=True)
    return moved.reshape(rows.shape)


def swap(array, distance, back=False):
    chips = lax.axis_size("z")
    pairs = []
    for z in range(chips):
        for core in range(2):
            to = (z + 2 * core - 1) % chips if distance > 1 else z
            pairs.append((2 * z + core, 2 * to + core ^ (distance % 2)))
    return lax.ppermute(array, HEAD, [(b, a) for a, b in pairs] if back else pairs)


def sum_over_head(keep, give):
    chips = lax.axis_size("z")
    spread = call(spread_kernel, shape(chips, *keep.shape), keep, swap(give, 1))
    moved = lax.all_to_all(spread, "z", split_axis=0, concat_axis=0, tiled=True)
    own = call(sum_kernel, shape(*keep.shape), moved)
    return own, swap(own, 1)


def per_device(latent, routes, gate_q, up_weight, down_weight, out_weight, cotangent):
    groups = lax.axis_size("expert")
    tokens, width = latent.shape
    unit = up_weight.shape[2]
    count = groups * ROWS
    half = shape(tokens, width // 2)
    half_wide = shape(tokens, width // 2, dtype=F32)
    me = (2 * (lax.axis_index("z") & 1) + lax.axis_index("core")).astype(jnp.int32).reshape(1)
    table = jnp.concatenate([routes, gate_q], axis=1).T

    packs = call(
        pack_kernel,
        [shape(2 * width, unit)] * (QUAD - 1),
        me, up_weight, down_weight, scalars=1,
    )
    packs = [swap(p, d) for d, p in enumerate(packs, 1)]

    back = call(
        back_kernel, [half_wide, half], me, cotangent, out_weight,
        scalars=1, flops=2 * tokens * width * cotangent.shape[1],
    )
    back = sum_over_head(*back)
    send, coef = call(
        send_kernel,
        [shape(count, width), shape(count, tokens)],
        me, table, latent, *back,
        scalars=1, out_hbm=(0,),
        scratch=[pltpu.VMEM((count, width), BF16), pltpu.SemaphoreType.DMA((CHUNKS,))],
    )
    rows = exchange(send, "expert")
    hidden = unit * QUAD
    copies = 3 + 2 * QUAD + (QUAD - 1) * (width // unit)
    out, *grads = call(
        expert_kernel,
        [shape(count, width // 2)] + [shape(width, unit)] * QUAD,
        me, rows, up_weight, down_weight, *packs,
        scalars=1, flops=8 * count * width * hidden,
        in_hbm=range(1, 4 + QUAD), out_hbm=range(QUAD + 1),
        scratch=[
            pltpu.VMEM((count, width), BF16),
            pltpu.VMEM((width, hidden), BF16),
            pltpu.VMEM((hidden, width), BF16),
            pltpu.VMEM((count, width // 2), BF16),
            pltpu.VMEM((width, hidden), BF16),
            pltpu.SemaphoreType.DMA((copies,)),
        ],
    )
    grads = [grads[0]] + [swap(g, d, back=True) for d, g in enumerate(grads[1:], 1)]
    returned = exchange(out, "expert")
    comb = call(combine_kernel, [half_wide, half], me, returned, coef, gate_q, scalars=1)
    comb = sum_over_head(*comb)
    mixed = call(
        mixed_kernel, shape(tokens, out_weight.shape[1]), me, *comb, out_weight,
        scalars=1, flops=2 * tokens * width * out_weight.shape[1],
    )
    grad_up = call(grad_kernel, shape(*up_weight.shape), me, *grads, scalars=1)
    return (mixed, grad_up)


def solution(mesh):
    groups, members = mesh.devices.shape
    fine = Mesh(mesh.devices.reshape(groups, members // 2, 2), ("expert", *HEAD))
    placed = (
        P("expert", None),
        P("expert", None),
        P("expert", None),
        P("expert", None, HEAD),
        P("expert", HEAD, None),
        P(None, HEAD),
        P("expert", HEAD),
    )
    return jax.shard_map(
        per_device,
        mesh=fine,
        in_specs=placed,
        out_specs=(P("expert", HEAD), P("expert", None, HEAD)),
        check_vma=False,
    )
```

```python
import jax
import jax.numpy as jnp
from jax import lax
from jax.experimental import pallas as pl
from jax.experimental.pallas import tpu as pltpu
from jax.sharding import Mesh, PartitionSpec as P

F32 = jnp.float32
BF16 = jnp.bfloat16
HEAD = ("z", "core")
QUAD = 4
CHUNKS = 4
MIB = 2**20
MOST = 4
ROWS = 2 * MOST
ANY = pl.BlockSpec(memory_space=pl.ANY)
VMEM = pl.BlockSpec(memory_space=pltpu.VMEM)
SMEM = pl.BlockSpec(memory_space=pltpu.SMEM)


def call(kernel, outs, *args, scalars=0, flops=0, in_hbm=(), out_hbm=(), scratch=(), vmem=32):
    single = not isinstance(outs, (list, tuple))
    moved = sum(a.size * a.dtype.itemsize for a in args)
    ins = [SMEM if i < scalars else ANY if i in in_hbm else VMEM for i in range(len(args))]
    places = [ANY if i in out_hbm else VMEM for i in range(1 if single else len(outs))]
    return pl.pallas_call(
        kernel,
        out_shape=outs,
        in_specs=ins,
        out_specs=places[0] if single else places,
        scratch_shapes=scratch,
        compiler_params=pltpu.CompilerParams(vmem_limit_bytes=vmem * MIB),
        cost_estimate=pl.CostEstimate(flops=flops, bytes_accessed=2 * moved, transcendentals=0),
    )(*args)


def shape(*dims, dtype=BF16):
    return jax.ShapeDtypeStruct(dims, dtype)


def dot(a, b, dims, precision=None):
    return lax.dot_general(a, b, (dims, ((), ())), precision=precision, preferred_element_type=F32)


def halves(me_ref, rows):
    half = rows.shape[1] // 2
    first = me_ref[0] % 2 == 0
    left, right = rows[:, :half], rows[:, half:]
    return jnp.where(first, left, right), jnp.where(first, right, left)


def joined(me_ref, own, other):
    first = me_ref[0] % 2 == 0
    own, other = own.astype(F32), other.astype(F32)
    return jnp.concatenate([jnp.where(first, own, other), jnp.where(first, other, own)], axis=1)


def back_kernel(me_ref, cot_hbm, out_w_hbm, keep_ref, give_ref, cot_ref, out_w_ref, sems):
    copies = [
        pltpu.make_async_copy(out_w_hbm, out_w_ref, sems.at[0]),
        pltpu.make_async_copy(cot_hbm, cot_ref, sems.at[1]),
    ]
    for copy in copies:
        copy.start()
    for copy in copies:
        copy.wait()
    part = dot(cot_ref[...], out_w_ref[...], ((1,), (1,)))
    keep, give = halves(me_ref, part)
    keep_ref[...] = keep
    give_ref[...] = give.astype(BF16)


def spread_kernel(keep_ref, got_ref, o_ref):
    rows = (keep_ref[...] + got_ref[...].astype(F32)).astype(BF16)
    for z in range(o_ref.shape[0]):
        o_ref[z] = rows


def sum_kernel(i_ref, o_ref):
    o_ref[...] = jnp.sum(i_ref[...].astype(F32), axis=0).astype(BF16)


def send_kernel(me_ref, table_ref, latent_ref, own_ref, other_ref, send_ref, coef_ref, buf, sems):
    count = send_ref.shape[0]
    tokens = latent_ref.shape[0]
    top = table_ref.shape[0] // 2
    step = count // CHUNKS
    back = joined(me_ref, own_ref[...], other_ref[...]).astype(BF16)
    latent = latent_ref[...]
    total = jnp.zeros((1, tokens), jnp.int32)
    for k in range(top):
        total = total + table_ref[top + k : top + k + 1, :]
    earlier = lax.broadcasted_iota(jnp.int32, (tokens, tokens), 0)
    later = lax.broadcasted_iota(jnp.int32, (tokens, tokens), 1)
    before = jnp.where(earlier < later, 1.0, 0.0).astype(BF16)
    is_latent = lax.broadcasted_iota(jnp.int32, (step, 1), 0) % ROWS < MOST
    copies = []
    for i in range(CHUNKS):
        at = pl.ds(step * i, step)
        row = lax.broadcasted_iota(jnp.int32, (step, tokens), 0) + step * i
        expert = QUAD * (row // ROWS) + me_ref[0]
        score = jnp.zeros((step, tokens), jnp.int32)
        for k in range(top):
            q = table_ref[top + k : top + k + 1, :]
            score = score + jnp.where(table_ref[k : k + 1, :] == expert, q, 0)
        score = score.astype(F32)
        named = score > 0.0
        rank = dot(jnp.where(named, 1.0, 0.0).astype(BF16), before, ((1,), (0,)))
        here = named & (rank == (row % MOST).astype(F32))
        coef_ref[at, :] = jnp.where(here, score, 0.0).astype(BF16)
        pick = jnp.where(here, 1.0, 0.0).astype(BF16)
        gate = jnp.sum(jnp.where(here, score / total.astype(F32), 0.0), axis=1, keepdims=True)
        latent_rows = dot(pick, latent, ((1,), (0,)))
        back_rows = dot(pick, back, ((1,), (0,)))
        buf[at, :] = jnp.where(is_latent, latent_rows, gate * back_rows).astype(BF16)
        copies.append(pltpu.make_async_copy(buf.at[at, :], send_ref.at[at, :], sems.at[i]))
        copies[-1].start()
    for copy in copies:
        copy.wait()


def pack_kernel(me_ref, up_ref, down_ref, *outs):
    width, unit = up_ref.shape[1], up_ref.shape[2]
    for d, o_ref in enumerate(outs, 1):
        expert = me_ref[0] ^ d
        o_ref[0:width, :] = up_ref[expert]
        for b in range(width // unit):
            o_ref[width + unit * b : width + unit * (b + 1), :] = down_ref[
                expert, :, unit * b : unit * (b + 1)
            ]


def expert_kernel(me_ref, rows_hbm, up_hbm, down_hbm, *refs):
    packs, refs = refs[: QUAD - 1], refs[QUAD - 1 :]
    out_hbm, *grads_hbm = refs[: QUAD + 1]
    rows_ref, up_ref, down_ref, out_ref, grad_ref, sems = refs[QUAD + 1 :]
    width, unit = up_hbm.shape[1], up_hbm.shape[2]
    count = rows_hbm.shape[0]
    half = width // 2
    me = me_ref[0]
    copies = []

    def fetch(source, target):
        copies.append(pltpu.make_async_copy(source, target, sems.at[len(copies)]))
        copies[-1].start()
        return copies[-1]

    first = [fetch(rows_hbm, rows_ref), fetch(up_hbm.at[me], up_ref.at[:, 0:unit])]
    for d, p in enumerate(packs, 1):
        at = pl.ds(unit * d, unit)
        first.append(fetch(p.at[pl.ds(0, width), :], up_ref.at[:, at]))
    second = [fetch(down_hbm.at[me], down_ref.at[0:unit, :])]
    for d, p in enumerate(packs, 1):
        at = pl.ds(unit * d, unit)
        for b in range(width // unit):
            block = p.at[pl.ds(width + unit * b, unit), :]
            second.append(fetch(block, down_ref.at[at, pl.ds(unit * b, unit)]))

    is_latent = lax.broadcasted_iota(jnp.int32, (count, 1), 0) % ROWS < MOST
    for copy in first:
        copy.wait()
    rows = rows_ref[...]
    act = jnp.maximum(dot(rows, up_ref[...], ((1,), (0,))), 0.0)
    hidden = act * act
    hidden = jnp.where(is_latent, hidden, pltpu.roll(hidden, MOST, 0)).astype(BF16)
    for copy in second:
        copy.wait()
    left = dot(hidden, down_ref[:, :half], ((1,), (0,)))
    right = dot(hidden, down_ref[:, half:], ((1,), (0,)))
    out_ref[...] = jnp.where(is_latent, left, right).astype(BF16)
    results = [fetch(out_ref, out_hbm)]
    hidden_grad = pltpu.roll(dot(rows, down_ref[...], ((1,), (1,))), count - MOST, 0)
    pre_grad = jnp.where(is_latent, hidden_grad * 2.0 * act, 0.0).astype(BF16)
    grad_ref[...] = dot(rows, pre_grad, ((0,), (0,))).astype(BF16)
    for d, g in enumerate(grads_hbm):
        results.append(fetch(grad_ref.at[:, pl.ds(unit * d, unit)], g))
    for copy in results:
        copy.wait()


def combine_kernel(me_ref, rows_ref, coef_ref, gate_ref, keep_ref, give_ref):
    count = rows_ref.shape[0]
    is_left = lax.broadcasted_iota(jnp.int32, (count, 1), 0) % ROWS < MOST
    coef = coef_ref[...].astype(F32)
    left = jnp.where(is_left, coef, 0.0).astype(BF16)
    right = jnp.where(is_left, 0.0, coef).astype(BF16)
    rows = rows_ref[...]
    total = jnp.sum(gate_ref[...].astype(F32), axis=1, keepdims=True)
    parts = [dot(c, rows, ((0,), (0,))) / total for c in (left, right)]
    keep, give = halves(me_ref, jnp.concatenate(parts, axis=1))
    keep_ref[...] = keep
    give_ref[...] = give.astype(BF16)


def mixed_kernel(me_ref, own_ref, other_ref, out_w_ref, o_ref):
    combined = joined(me_ref, own_ref[...], other_ref[...]).astype(BF16)
    o_ref[...] = dot(combined, out_w_ref[...], ((1,), (0,))).astype(BF16)


def grad_kernel(me_ref, *refs):
    grads, o_ref = refs[:-1], refs[-1]
    for d, g_ref in enumerate(grads):
        o_ref[me_ref[0] ^ d] = g_ref[...]


def exchange(rows, axis):
    peers = lax.axis_size(axis)
    split = rows.reshape(peers, rows.shape[0] // peers, rows.shape[1])
    moved = lax.all_to_all(split, axis, split_axis=0, concat_axis=0, tiled=True)
    return moved.reshape(rows.shape)


def swap(array, distance, back=False):
    chips = lax.axis_size("z")
    pairs = []
    for z in range(chips):
        for core in range(2):
            to = (z + 2 * core - 1) % chips if distance > 1 else z
            pairs.append((2 * z + core, 2 * to + core ^ (distance % 2)))
    return lax.ppermute(array, HEAD, [(b, a) for a, b in pairs] if back else pairs)


def sum_over_head(keep, give):
    chips = lax.axis_size("z")
    spread = call(spread_kernel, shape(chips, *keep.shape), keep, swap(give, 1))
    moved = lax.all_to_all(spread, "z", split_axis=0, concat_axis=0, tiled=True)
    own = call(sum_kernel, shape(*keep.shape), moved)
    return own, swap(own, 1)


def per_device(latent, routes, gate_q, up_weight, down_weight, out_weight, cotangent):
    groups = lax.axis_size("expert")
    tokens, width = latent.shape
    unit = up_weight.shape[2]
    count = groups * ROWS
    half = shape(tokens, width // 2)
    half_wide = shape(tokens, width // 2, dtype=F32)
    me = (2 * (lax.axis_index("z") & 1) + lax.axis_index("core")).astype(jnp.int32).reshape(1)
    table = jnp.concatenate([routes, gate_q], axis=1).T

    packs = call(
        pack_kernel,
        [shape(2 * width, unit)] * (QUAD - 1),
        me, up_weight, down_weight, scalars=1,
    )
    packs = [swap(p, d) for d, p in enumerate(packs, 1)]

    back = call(
        back_kernel, [half_wide, half], me, cotangent, out_weight,
        scalars=1, flops=2 * tokens * width * cotangent.shape[1], in_hbm=(1, 2), vmem=53,
        scratch=[
            pltpu.VMEM(cotangent.shape, BF16),
            pltpu.VMEM(out_weight.shape, BF16),
            pltpu.SemaphoreType.DMA((2,)),
        ],
    )
    back = sum_over_head(*back)
    send, coef = call(
        send_kernel,
        [shape(count, width), shape(count, tokens)],
        me, table, latent, *back,
        scalars=1, out_hbm=(0,), vmem=53,
        scratch=[pltpu.VMEM((count, width), BF16), pltpu.SemaphoreType.DMA((CHUNKS,))],
    )
    rows = exchange(send, "expert")
    hidden = unit * QUAD
    copies = 3 + 2 * QUAD + (QUAD - 1) * (width // unit)
    out, *grads = call(
        expert_kernel,
        [shape(count, width // 2)] + [shape(width, unit)] * QUAD,
        me, rows, up_weight, down_weight, *packs,
        scalars=1, flops=8 * count * width * hidden,
        in_hbm=range(1, 4 + QUAD), out_hbm=range(QUAD + 1), vmem=49,
        scratch=[
            pltpu.VMEM((count, width), BF16),
            pltpu.VMEM((width, hidden), BF16),
            pltpu.VMEM((hidden, width), BF16),
            pltpu.VMEM((count, width // 2), BF16),
            pltpu.VMEM((width, hidden), BF16),
            pltpu.SemaphoreType.DMA((copies,)),
        ],
    )
    grads = [grads[0]] + [swap(g, d, back=True) for d, g in enumerate(grads[1:], 1)]
    grad_up = call(grad_kernel, shape(*up_weight.shape), me, *grads, scalars=1)
    returned, grad_up = lax.optimization_barrier((exchange(out, "expert"), grad_up))
    comb = call(combine_kernel, [half_wide, half], me, returned, coef, gate_q, scalars=1)
    comb = sum_over_head(*comb)
    mixed = call(
        mixed_kernel, shape(tokens, out_weight.shape[1]), me, *comb, out_weight,
        scalars=1, flops=2 * tokens * width * out_weight.shape[1],
    )
    return (mixed, grad_up)


def solution(mesh):
    groups, members = mesh.devices.shape
    fine = Mesh(mesh.devices.reshape(groups, members // 2, 2), ("expert", *HEAD))
    placed = (
        P("expert", None),
        P("expert", None),
        P("expert", None),
        P("expert", None, HEAD),
        P("expert", HEAD, None),
        P(None, HEAD),
        P("expert", HEAD),
    )
    return jax.shard_map(
        per_device,
        mesh=fine,
        in_specs=placed,
        out_specs=(P("expert", HEAD), P("expert", None, HEAD)),
        check_vma=False,
    )
```

```python
import jax
import jax.numpy as jnp
from jax import lax
from jax.experimental import pallas as pl
from jax.experimental.pallas import tpu as pltpu
from jax.sharding import Mesh, PartitionSpec as P

F32 = jnp.float32
BF16 = jnp.bfloat16
HEAD = ("z", "core")
QUAD = 4
VMEM_LARGE = 49
MIB = 2**20
MOST = 4
ROWS = 2 * MOST
ANY = pl.BlockSpec(memory_space=pl.ANY)
VMEM = pl.BlockSpec(memory_space=pltpu.VMEM)
SMEM = pl.BlockSpec(memory_space=pltpu.SMEM)


def call(kernel, outs, *args, scalars=0, flops=0, in_hbm=(), out_hbm=(), scratch=(), vmem=32):
    single = not isinstance(outs, (list, tuple))
    moved = sum(a.size * a.dtype.itemsize for a in args)
    ins = [SMEM if i < scalars else ANY if i in in_hbm else VMEM for i in range(len(args))]
    places = [ANY if i in out_hbm else VMEM for i in range(1 if single else len(outs))]
    return pl.pallas_call(
        kernel,
        out_shape=outs,
        in_specs=ins,
        out_specs=places[0] if single else places,
        scratch_shapes=scratch,
        compiler_params=pltpu.CompilerParams(vmem_limit_bytes=vmem * MIB),
        cost_estimate=pl.CostEstimate(flops=flops, bytes_accessed=2 * moved, transcendentals=0),
    )(*args)


def shape(*dims, dtype=BF16):
    return jax.ShapeDtypeStruct(dims, dtype)


def dot(a, b, dims, precision=None):
    return lax.dot_general(a, b, (dims, ((), ())), precision=precision, preferred_element_type=F32)


def halves(me_ref, rows):
    half = rows.shape[1] // 2
    first = me_ref[0] % 2 == 0
    left, right = rows[:, :half], rows[:, half:]
    return jnp.where(first, left, right), jnp.where(first, right, left)


def joined(me_ref, own, other):
    first = me_ref[0] % 2 == 0
    own, other = own.astype(F32), other.astype(F32)
    return jnp.concatenate([jnp.where(first, own, other), jnp.where(first, other, own)], axis=1)


def back_kernel(me_ref, cot_hbm, out_w_hbm, keep_ref, give_ref, cot_ref, out_w_ref, sems):
    copies = [
        pltpu.make_async_copy(out_w_hbm, out_w_ref, sems.at[0]),
        pltpu.make_async_copy(cot_hbm, cot_ref, sems.at[1]),
    ]
    for copy in copies:
        copy.start()
    for copy in copies:
        copy.wait()
    part = dot(cot_ref[...], out_w_ref[...], ((1,), (1,)))
    keep, give = halves(me_ref, part)
    keep_ref[...] = keep
    give_ref[...] = give.astype(BF16)


def spread_kernel(keep_ref, got_ref, o_ref):
    rows = (keep_ref[...] + got_ref[...].astype(F32)).astype(BF16)
    for z in range(o_ref.shape[0]):
        o_ref[z] = rows


def sum_kernel(i_ref, o_ref):
    o_ref[...] = jnp.sum(i_ref[...].astype(F32), axis=0).astype(BF16)


def left_half(count):
    return lax.broadcasted_iota(jnp.int32, (count, 1), 0) % ROWS < MOST


def latent_kernel(me_ref, table_ref, latent_ref, send_ref, coef_ref):
    count, half = send_ref.shape
    tokens = latent_ref.shape[0]
    top = table_ref.shape[0] // 2
    row = lax.broadcasted_iota(jnp.int32, (count, tokens), 0)
    expert = QUAD * (row // ROWS) + me_ref[0]
    score = jnp.zeros((count, tokens), jnp.int32)
    for k in range(top):
        q = table_ref[top + k : top + k + 1, :]
        score = score + jnp.where(table_ref[k : k + 1, :] == expert, q, 0)
    score = score.astype(F32)
    named = score > 0.0
    earlier = lax.broadcasted_iota(jnp.int32, (tokens, tokens), 0)
    later = lax.broadcasted_iota(jnp.int32, (tokens, tokens), 1)
    before = jnp.where(earlier < later, 1.0, 0.0).astype(BF16)
    rank = dot(jnp.where(named, 1.0, 0.0).astype(BF16), before, ((1,), (0,)))
    here = named & (rank == (row % MOST).astype(F32))
    coef_ref[...] = jnp.where(here, score, 0.0).astype(BF16)
    pick = jnp.where(here, 1.0, 0.0).astype(BF16)
    left = dot(pick, latent_ref[:, :half], ((1,), (0,)))
    right = dot(pick, latent_ref[:, half:], ((1,), (0,)))
    send_ref[...] = jnp.where(left_half(count), left, right).astype(BF16)


def gradient_kernel(me_ref, table_ref, coef_ref, own_ref, other_ref, send_ref):
    top = table_ref.shape[0] // 2
    first = me_ref[0] % 2 == 0
    coef = coef_ref[...].astype(F32)
    total = jnp.sum(table_ref[top:, :].astype(F32), axis=0, keepdims=True)
    gate = jnp.sum(coef / total, axis=1, keepdims=True)
    pick = jnp.where(coef > 0.0, 1.0, 0.0).astype(BF16)
    own = dot(pick, own_ref[...], ((1,), (0,)))
    other = dot(pick, other_ref[...], ((1,), (0,)))
    rows = jnp.where(left_half(coef.shape[0]) == first, own, other)
    send_ref[...] = (gate * rows).astype(BF16)


def pack_kernel(me_ref, up_ref, down_ref, *outs):
    width, unit = up_ref.shape[1], up_ref.shape[2]
    for d, o_ref in enumerate(outs, 1):
        expert = me_ref[0] ^ d
        o_ref[0:width, :] = up_ref[expert]
        for b in range(width // unit):
            o_ref[width + unit * b : width + unit * (b + 1), :] = down_ref[
                expert, :, unit * b : unit * (b + 1)
            ]


class Copies:
    def __init__(self, sems):
        self.sems, self.used = sems, 0

    def start(self, source, target):
        copy = pltpu.make_async_copy(source, target, self.sems.at[self.used])
        self.used += 1
        copy.start()
        return copy

    def start_down(self, me, down_hbm, packs, down_ref):
        unit, width = down_hbm.shape[1:]
        started = [self.start(down_hbm.at[me], down_ref.at[0:unit, :])]
        for d, p in enumerate(packs, 1):
            at = pl.ds(unit * d, unit)
            for b in range(width // unit):
                block = p.at[pl.ds(width + unit * b, unit), :]
                started.append(self.start(block, down_ref.at[at, pl.ds(unit * b, unit)]))
        return started


def wait(copies):
    for copy in copies:
        copy.wait()


def forward_kernel(me_ref, rows_hbm, up_hbm, down_hbm, *refs):
    packs, refs = refs[: QUAD - 1], refs[QUAD - 1 :]
    out_hbm, act_hbm, rows_ref, up_ref, down_ref, out_ref, act_ref, sems = refs
    width, unit = up_hbm.shape[1], up_hbm.shape[2]
    count, half = rows_hbm.shape
    me = me_ref[0]
    copies = Copies(sems)
    first = [copies.start(rows_hbm, rows_ref), copies.start(up_hbm.at[me], up_ref.at[:, 0:unit])]
    for d, p in enumerate(packs, 1):
        at = pl.ds(unit * d, unit)
        first.append(copies.start(p.at[pl.ds(0, width), :], up_ref.at[:, at]))
    second = copies.start_down(me, down_hbm, packs, down_ref)
    is_left = left_half(count)
    wait(first)
    rows = rows_ref[...]
    right = pltpu.roll(dot(rows, up_ref[half:, :], ((1,), (0,))), count - MOST, 0)
    act = jnp.maximum(dot(rows, up_ref[:half, :], ((1,), (0,))) + right, 0.0)
    act_ref[...] = act
    third = [copies.start(act_ref, act_hbm)]
    hidden = act * act
    hidden = jnp.where(is_left, hidden, pltpu.roll(hidden, MOST, 0)).astype(BF16)
    wait(second)
    left = dot(hidden, down_ref[:, :half], ((1,), (0,)))
    right = dot(hidden, down_ref[:, half:], ((1,), (0,)))
    out_ref[...] = jnp.where(is_left, left, right).astype(BF16)
    third.append(copies.start(out_ref, out_hbm))
    wait(third)


def weight_kernel(me_ref, rows_hbm, grads_hbm, act_hbm, down_hbm, *refs):
    packs, refs = refs[: QUAD - 1], refs[QUAD - 1 :]
    outs_hbm, refs = refs[:QUAD], refs[QUAD:]
    rows_ref, grads_ref, act_ref, down_ref, out_ref, sems = refs
    unit = down_hbm.shape[1]
    count, half = rows_hbm.shape
    copies = Copies(sems)
    first = [copies.start(grads_hbm, grads_ref)]
    first += copies.start_down(me_ref[0], down_hbm, packs, down_ref)
    first += [copies.start(act_hbm, act_ref), copies.start(rows_hbm, rows_ref)]
    wait(first)
    grads = grads_ref[...]
    right = pltpu.roll(dot(grads, down_ref[:, half:], ((1,), (1,))), count - MOST, 0)
    hidden_grad = dot(grads, down_ref[:, :half], ((1,), (1,))) + right
    pre_grad = jnp.where(left_half(count), hidden_grad * 2.0 * act_ref[...], 0.0)
    rows = rows_ref[...]
    out_ref[:half, :] = dot(rows, pre_grad.astype(BF16), ((0,), (0,))).astype(BF16)
    lower = pltpu.roll(pre_grad, MOST, 0).astype(BF16)
    out_ref[half:, :] = dot(rows, lower, ((0,), (0,))).astype(BF16)
    wait([copies.start(out_ref.at[:, pl.ds(unit * d, unit)], o) for d, o in enumerate(outs_hbm)])


def combine_kernel(me_ref, rows_ref, coef_ref, gate_ref, keep_ref, give_ref):
    count = rows_ref.shape[0]
    is_left = lax.broadcasted_iota(jnp.int32, (count, 1), 0) % ROWS < MOST
    coef = coef_ref[...].astype(F32)
    left = jnp.where(is_left, coef, 0.0).astype(BF16)
    right = jnp.where(is_left, 0.0, coef).astype(BF16)
    rows = rows_ref[...]
    total = jnp.sum(gate_ref[...].astype(F32), axis=1, keepdims=True)
    parts = [dot(c, rows, ((0,), (0,))) / total for c in (left, right)]
    keep, give = halves(me_ref, jnp.concatenate(parts, axis=1))
    keep_ref[...] = keep
    give_ref[...] = give.astype(BF16)


def mixed_kernel(me_ref, own_ref, other_ref, out_w_ref, o_ref):
    combined = joined(me_ref, own_ref[...], other_ref[...]).astype(BF16)
    o_ref[...] = dot(combined, out_w_ref[...], ((1,), (0,))).astype(BF16)


def grad_kernel(me_ref, *refs):
    grads, o_ref = refs[:-1], refs[-1]
    for d, g_ref in enumerate(grads):
        o_ref[me_ref[0] ^ d] = g_ref[...]


def exchange(rows, axis):
    peers = lax.axis_size(axis)
    split = rows.reshape(peers, rows.shape[0] // peers, rows.shape[1])
    moved = lax.all_to_all(split, axis, split_axis=0, concat_axis=0, tiled=True)
    return moved.reshape(rows.shape)


def swap(array, distance, back=False):
    chips = lax.axis_size("z")
    pairs = []
    for z in range(chips):
        for core in range(2):
            to = (z + 2 * core - 1) % chips if distance > 1 else z
            pairs.append((2 * z + core, 2 * to + core ^ (distance % 2)))
    return lax.ppermute(array, HEAD, [(b, a) for a, b in pairs] if back else pairs)


def sum_over_head(keep, give):
    chips = lax.axis_size("z")
    spread = call(spread_kernel, shape(chips, *keep.shape), keep, swap(give, 1))
    moved = lax.all_to_all(spread, "z", split_axis=0, concat_axis=0, tiled=True)
    own = call(sum_kernel, shape(*keep.shape), moved)
    return own, swap(own, 1)


def per_device(latent, routes, gate_q, up_weight, down_weight, out_weight, cotangent):
    groups = lax.axis_size("expert")
    tokens, width = latent.shape
    unit = up_weight.shape[2]
    count = groups * ROWS
    half = shape(tokens, width // 2)
    half_wide = shape(tokens, width // 2, dtype=F32)
    me = (2 * (lax.axis_index("z") & 1) + lax.axis_index("core")).astype(jnp.int32).reshape(1)
    table = jnp.concatenate([routes, gate_q], axis=1).T

    send, coef = call(
        latent_kernel,
        [shape(count, width // 2), shape(count, tokens)],
        me, table, latent, scalars=1, vmem=53,
    )
    packs = call(
        pack_kernel,
        [shape(2 * width, unit)] * (QUAD - 1),
        me, up_weight, down_weight, scalars=1,
    )
    packs = [swap(p, d) for d, p in enumerate(packs, 1)]

    back = call(
        back_kernel, [half_wide, half], me, cotangent, out_weight,
        scalars=1, flops=2 * tokens * width * cotangent.shape[1], in_hbm=(1, 2), vmem=53,
        scratch=[
            pltpu.VMEM(cotangent.shape, BF16),
            pltpu.VMEM(out_weight.shape, BF16),
            pltpu.SemaphoreType.DMA((2,)),
        ],
    )
    back = sum_over_head(*back)
    hidden = unit * QUAD
    swapped = (QUAD - 1) * (width // unit)
    wide = pltpu.VMEM((count, width // 2), BF16)
    up_space, down_space = pltpu.VMEM((width, hidden), BF16), pltpu.VMEM((hidden, width), BF16)
    act_space = pltpu.VMEM((count, hidden), F32)
    grad_send = call(
        gradient_kernel, shape(count, width // 2), me, table, coef, *back, scalars=1, vmem=53
    )
    rows = exchange(send, "expert")
    out, act = call(
        forward_kernel,
        [shape(count, width // 2), shape(count, hidden, dtype=F32)],
        me, rows, up_weight, down_weight, *packs,
        scalars=1, flops=4 * count * width * hidden,
        in_hbm=range(1, 4 + QUAD), out_hbm=range(2), vmem=VMEM_LARGE,
        scratch=[wide, up_space, down_space, wide, act_space, pltpu.SemaphoreType.DMA((4 + QUAD + swapped,))],
    )
    grad_rows = exchange(grad_send, "expert")
    grads = call(
        weight_kernel,
        [shape(width, unit)] * QUAD,
        me, rows, grad_rows, act, down_weight, *packs,
        scalars=1, flops=4 * count * width * hidden,
        in_hbm=range(1, 5 + QUAD), out_hbm=range(QUAD), vmem=VMEM_LARGE,
        scratch=[wide, wide, act_space, down_space, up_space, pltpu.SemaphoreType.DMA((4 + QUAD + swapped,))],
    )
    grads = [grads[0]] + [swap(g, d, back=True) for d, g in enumerate(grads[1:], 1)]
    grad_up = call(grad_kernel, shape(*up_weight.shape), me, *grads, scalars=1)
    returned = exchange(out, "expert")
    comb = call(combine_kernel, [half_wide, half], me, returned, coef, gate_q, scalars=1)
    comb = sum_over_head(*comb)
    mixed = call(
        mixed_kernel, shape(tokens, out_weight.shape[1]), me, *comb, out_weight,
        scalars=1, flops=2 * tokens * width * out_weight.shape[1],
    )
    return (mixed, grad_up)


def solution(mesh):
    groups, members = mesh.devices.shape
    fine = Mesh(mesh.devices.reshape(groups, members // 2, 2), ("expert", *HEAD))
    placed = (
        P("expert", None),
        P("expert", None),
        P("expert", None),
        P("expert", None, HEAD),
        P("expert", HEAD, None),
        P(None, HEAD),
        P("expert", HEAD),
    )
    return jax.shard_map(
        per_device,
        mesh=fine,
        in_specs=placed,
        out_specs=(P("expert", HEAD), P("expert", None, HEAD)),
        check_vma=False,
    )
```

```python
import jax
import jax.numpy as jnp
from jax import lax
from jax.experimental import pallas as pl
from jax.experimental.pallas import tpu as pltpu
from jax.sharding import Mesh, PartitionSpec as P

F32 = jnp.float32
BF16 = jnp.bfloat16
HEAD = ("z", "core")
QUAD = 4
CHUNKS = 4
BACK_VMEM, SEND_VMEM, FORWARD_VMEM, WEIGHT_VMEM = 53, 53, 50, 50
MIB = 2**20
MOST = 4
ROWS = 2 * MOST
ANY = pl.BlockSpec(memory_space=pl.ANY)
VMEM = pl.BlockSpec(memory_space=pltpu.VMEM)
SMEM = pl.BlockSpec(memory_space=pltpu.SMEM)


def call(kernel, outs, *args, scalars=0, flops=0, in_hbm=(), out_hbm=(), scratch=(), vmem=32):
    single = not isinstance(outs, (list, tuple))
    moved = sum(a.size * a.dtype.itemsize for a in args)
    ins = [SMEM if i < scalars else ANY if i in in_hbm else VMEM for i in range(len(args))]
    places = [ANY if i in out_hbm else VMEM for i in range(1 if single else len(outs))]
    return pl.pallas_call(
        kernel,
        out_shape=outs,
        in_specs=ins,
        out_specs=places[0] if single else places,
        scratch_shapes=scratch,
        compiler_params=pltpu.CompilerParams(vmem_limit_bytes=vmem * MIB),
        cost_estimate=pl.CostEstimate(flops=flops, bytes_accessed=2 * moved, transcendentals=0),
    )(*args)


def shape(*dims, dtype=BF16):
    return jax.ShapeDtypeStruct(dims, dtype)


def dot(a, b, dims, precision=None):
    return lax.dot_general(a, b, (dims, ((), ())), precision=precision, preferred_element_type=F32)


def halves(me_ref, rows):
    half = rows.shape[1] // 2
    first = me_ref[0] % 2 == 0
    left, right = rows[:, :half], rows[:, half:]
    return jnp.where(first, left, right), jnp.where(first, right, left)


def joined(me_ref, own, other):
    first = me_ref[0] % 2 == 0
    own, other = own.astype(F32), other.astype(F32)
    return jnp.concatenate([jnp.where(first, own, other), jnp.where(first, other, own)], axis=1)


def back_kernel(me_ref, cot_hbm, out_w_hbm, keep_ref, give_ref, cot_ref, out_w_ref, sems):
    copies = [
        pltpu.make_async_copy(out_w_hbm, out_w_ref, sems.at[0]),
        pltpu.make_async_copy(cot_hbm, cot_ref, sems.at[1]),
    ]
    for copy in copies:
        copy.start()
    for copy in copies:
        copy.wait()
    part = dot(cot_ref[...], out_w_ref[...], ((1,), (1,)))
    keep, give = halves(me_ref, part)
    keep_ref[...] = keep
    give_ref[...] = give.astype(BF16)


def spread_kernel(keep_ref, got_ref, o_ref):
    rows = (keep_ref[...] + got_ref[...].astype(F32)).astype(BF16)
    for z in range(o_ref.shape[0]):
        o_ref[z] = rows


def sum_kernel(i_ref, o_ref):
    o_ref[...] = jnp.sum(i_ref[...].astype(F32), axis=0).astype(BF16)


def pick_kernel(me_ref, table_ref, coef_ref):
    count, tokens = coef_ref.shape
    top = table_ref.shape[0] // 2
    row = lax.broadcasted_iota(jnp.int32, (count, tokens), 0)
    expert = QUAD * (row // ROWS) + me_ref[0]
    score = jnp.zeros((count, tokens), jnp.int32)
    for k in range(top):
        q = table_ref[top + k : top + k + 1, :]
        score = score + jnp.where(table_ref[k : k + 1, :] == expert, q, 0)
    score = score.astype(F32)
    named = score > 0.0
    earlier = lax.broadcasted_iota(jnp.int32, (tokens, tokens), 0)
    later = lax.broadcasted_iota(jnp.int32, (tokens, tokens), 1)
    before = jnp.where(earlier < later, 1.0, 0.0).astype(BF16)
    rank = dot(jnp.where(named, 1.0, 0.0).astype(BF16), before, ((1,), (0,)))
    here = named & (rank == (row % MOST).astype(F32))
    coef_ref[...] = jnp.where(here, score, 0.0).astype(BF16)


def send_kernel(me_ref, table_ref, coef_ref, latent_ref, own_ref, other_ref, send_ref, buf, sems):
    count = send_ref.shape[0]
    top = table_ref.shape[0] // 2
    step = count // CHUNKS
    back = joined(me_ref, own_ref[...], other_ref[...]).astype(BF16)
    latent = latent_ref[...]
    total = jnp.sum(table_ref[top:, :].astype(F32), axis=0, keepdims=True)
    is_latent = lax.broadcasted_iota(jnp.int32, (step, 1), 0) % ROWS < MOST
    copies = []
    for i in range(CHUNKS):
        at = pl.ds(step * i, step)
        coef = coef_ref[at, :].astype(F32)
        gate = jnp.sum(coef / total, axis=1, keepdims=True)
        pick = jnp.where(coef > 0.0, 1.0, 0.0).astype(BF16)
        latent_rows = dot(pick, latent, ((1,), (0,)))
        back_rows = dot(pick, back, ((1,), (0,)))
        buf[at, :] = jnp.where(is_latent, latent_rows, gate * back_rows).astype(BF16)
        copies.append(pltpu.make_async_copy(buf.at[at, :], send_ref.at[at, :], sems.at[i]))
        copies[-1].start()
    for copy in copies:
        copy.wait()


def pack_kernel(me_ref, up_ref, down_ref, *outs):
    width, unit = up_ref.shape[1], up_ref.shape[2]
    for d, o_ref in enumerate(outs, 1):
        expert = me_ref[0] ^ d
        o_ref[0:width, :] = up_ref[expert]
        for b in range(width // unit):
            o_ref[width + unit * b : width + unit * (b + 1), :] = down_ref[
                expert, :, unit * b : unit * (b + 1)
            ]


class Copies:
    def __init__(self, sems):
        self.sems, self.used = sems, 0

    def start(self, source, target):
        copy = pltpu.make_async_copy(source, target, self.sems.at[self.used])
        self.used += 1
        copy.start()
        return copy

    def start_down(self, me, down_hbm, packs, down_ref):
        unit, width = down_hbm.shape[1:]
        started = [self.start(down_hbm.at[me], down_ref.at[0:unit, :])]
        for d, p in enumerate(packs, 1):
            at = pl.ds(unit * d, unit)
            for b in range(width // unit):
                block = p.at[pl.ds(width + unit * b, unit), :]
                started.append(self.start(block, down_ref.at[at, pl.ds(unit * b, unit)]))
        return started

    def start_up(self, me, up_hbm, packs, up_ref):
        width, unit = up_hbm.shape[1:]
        started = [self.start(up_hbm.at[me], up_ref.at[:, 0:unit])]
        for d, p in enumerate(packs, 1):
            started.append(self.start(p.at[pl.ds(0, width), :], up_ref.at[:, pl.ds(unit * d, unit)]))
        return started


def wait(copies):
    for copy in copies:
        copy.wait()


def latent_rows_of(count):
    return lax.broadcasted_iota(jnp.int32, (count, 1), 0) % ROWS < MOST


def forward_kernel(me_ref, rows_ref, up_hbm, down_hbm, *refs):
    packs, refs = refs[: QUAD - 1], refs[QUAD - 1 :]
    out_hbm, up_ref, down_ref, out_ref, sems = refs
    count, half = out_ref.shape
    copies = Copies(sems)
    ups = copies.start_up(me_ref[0], up_hbm, packs, up_ref)
    downs = copies.start_down(me_ref[0], down_hbm, packs, down_ref)
    is_latent = latent_rows_of(count)
    wait(ups)
    act = jnp.maximum(dot(rows_ref[...], up_ref[...], ((1,), (0,))), 0.0)
    hidden = act * act
    hidden = jnp.where(is_latent, hidden, pltpu.roll(hidden, MOST, 0)).astype(BF16)
    wait(downs)
    left = dot(hidden, down_ref[:, :half], ((1,), (0,)))
    right = dot(hidden, down_ref[:, half:], ((1,), (0,)))
    out_ref[...] = jnp.where(is_latent, left, right).astype(BF16)
    wait([copies.start(out_ref, out_hbm)])


def weight_kernel(me_ref, rows_ref, up_hbm, down_hbm, *refs):
    packs, refs = refs[: QUAD - 1], refs[QUAD - 1 :]
    outs_hbm, refs = refs[:QUAD], refs[QUAD:]
    up_ref, down_ref, grad_ref, sems = refs
    unit = up_hbm.shape[2]
    count = rows_ref.shape[0]
    copies = Copies(sems)
    ups = copies.start_up(me_ref[0], up_hbm, packs, up_ref)
    downs = copies.start_down(me_ref[0], down_hbm, packs, down_ref)
    wait(ups)
    rows = rows_ref[...]
    act = jnp.maximum(dot(rows, up_ref[...], ((1,), (0,))), 0.0)
    wait(downs)
    hidden_grad = pltpu.roll(dot(rows, down_ref[...], ((1,), (1,))), count - MOST, 0)
    pre_grad = jnp.where(latent_rows_of(count), hidden_grad * 2.0 * act, 0.0).astype(BF16)
    grad_ref[...] = dot(rows, pre_grad, ((0,), (0,))).astype(BF16)
    wait([copies.start(grad_ref.at[:, pl.ds(unit * d, unit)], o) for d, o in enumerate(outs_hbm)])


def combine_kernel(me_ref, rows_ref, coef_ref, gate_ref, keep_ref, give_ref):
    count = rows_ref.shape[0]
    is_left = lax.broadcasted_iota(jnp.int32, (count, 1), 0) % ROWS < MOST
    coef = coef_ref[...].astype(F32)
    left = jnp.where(is_left, coef, 0.0).astype(BF16)
    right = jnp.where(is_left, 0.0, coef).astype(BF16)
    rows = rows_ref[...]
    total = jnp.sum(gate_ref[...].astype(F32), axis=1, keepdims=True)
    parts = [dot(c, rows, ((0,), (0,))) / total for c in (left, right)]
    keep, give = halves(me_ref, jnp.concatenate(parts, axis=1))
    keep_ref[...] = keep
    give_ref[...] = give.astype(BF16)


def mixed_kernel(me_ref, own_ref, other_ref, out_w_ref, o_ref):
    combined = joined(me_ref, own_ref[...], other_ref[...]).astype(BF16)
    o_ref[...] = dot(combined, out_w_ref[...], ((1,), (0,))).astype(BF16)


def grad_kernel(me_ref, *refs):
    grads, o_ref = refs[:-1], refs[-1]
    for d, g_ref in enumerate(grads):
        o_ref[me_ref[0] ^ d] = g_ref[...]


def exchange(rows, axis):
    peers = lax.axis_size(axis)
    split = rows.reshape(peers, rows.shape[0] // peers, rows.shape[1])
    moved = lax.all_to_all(split, axis, split_axis=0, concat_axis=0, tiled=True)
    return moved.reshape(rows.shape)


def swap(array, distance, back=False):
    chips = lax.axis_size("z")
    pairs = []
    for z in range(chips):
        for core in range(2):
            to = (z + 2 * core - 1) % chips if distance > 1 else z
            pairs.append((2 * z + core, 2 * to + core ^ (distance % 2)))
    return lax.ppermute(array, HEAD, [(b, a) for a, b in pairs] if back else pairs)


def sum_over_head(keep, give, beside=()):
    chips = lax.axis_size("z")
    spread = call(spread_kernel, shape(chips, *keep.shape), keep, swap(give, 1))
    moved = lax.all_to_all(spread, "z", split_axis=0, concat_axis=0, tiled=True)
    moved, *beside = lax.optimization_barrier((moved, *beside))
    own = call(sum_kernel, shape(*keep.shape), moved)
    return own, swap(own, 1), *beside


def per_device(latent, routes, gate_q, up_weight, down_weight, out_weight, cotangent):
    groups = lax.axis_size("expert")
    tokens, width = latent.shape
    unit = up_weight.shape[2]
    count = groups * ROWS
    half = shape(tokens, width // 2)
    half_wide = shape(tokens, width // 2, dtype=F32)
    me = (2 * (lax.axis_index("z") & 1) + lax.axis_index("core")).astype(jnp.int32).reshape(1)
    table = jnp.concatenate([routes, gate_q], axis=1).T

    coef = call(pick_kernel, shape(count, tokens), me, table, scalars=1)
    packs = call(
        pack_kernel,
        [shape(2 * width, unit)] * (QUAD - 1),
        me, up_weight, down_weight, scalars=1,
    )
    packs = [swap(p, d) for d, p in enumerate(packs, 1)]

    back = call(
        back_kernel, [half_wide, half], me, cotangent, out_weight,
        scalars=1, flops=2 * tokens * width * cotangent.shape[1], in_hbm=(1, 2), vmem=BACK_VMEM,
        scratch=[
            pltpu.VMEM(cotangent.shape, BF16),
            pltpu.VMEM(out_weight.shape, BF16),
            pltpu.SemaphoreType.DMA((2,)),
        ],
    )
    *back, table, coef = sum_over_head(*back, beside=(table, coef))
    send = call(
        send_kernel,
        shape(count, width),
        me, table, coef, latent, *back,
        scalars=1, out_hbm=(0,), vmem=SEND_VMEM,
        scratch=[pltpu.VMEM((count, width), BF16), pltpu.SemaphoreType.DMA((CHUNKS,))],
    )
    rows = exchange(send, "expert")
    hidden = unit * QUAD
    copies = 2 * QUAD + 1 + (QUAD - 1) * (width // unit)
    up_space, down_space = pltpu.VMEM((width, hidden), BF16), pltpu.VMEM((hidden, width), BF16)
    out = call(
        forward_kernel,
        shape(count, width // 2),
        me, rows, up_weight, down_weight, *packs,
        scalars=1, flops=4 * count * width * hidden,
        in_hbm=range(2, 4 + QUAD), out_hbm=(0,), vmem=FORWARD_VMEM,
        scratch=[
            up_space, down_space,
            pltpu.VMEM((count, width // 2), BF16), pltpu.SemaphoreType.DMA((copies,)),
        ],
    )
    grads = call(
        weight_kernel,
        [shape(width, unit)] * QUAD,
        me, rows, up_weight, down_weight, *packs,
        scalars=1, flops=6 * count * width * hidden,
        in_hbm=range(2, 4 + QUAD), out_hbm=range(QUAD), vmem=WEIGHT_VMEM,
        scratch=[up_space, down_space, up_space, pltpu.SemaphoreType.DMA((copies + QUAD,))],
    )
    grads = [grads[0]] + [swap(g, d, back=True) for d, g in enumerate(grads[1:], 1)]
    returned, *grads[1:3] = lax.optimization_barrier((exchange(out, "expert"), *grads[1:3]))
    grad_up = call(grad_kernel, shape(*up_weight.shape), me, *grads, scalars=1)
    comb = call(combine_kernel, [half_wide, half], me, returned, coef, gate_q, scalars=1)
    comb = sum_over_head(*comb)
    mixed = call(
        mixed_kernel, shape(tokens, out_weight.shape[1]), me, *comb, out_weight,
        scalars=1, flops=2 * tokens * width * out_weight.shape[1],
    )
    return (mixed, grad_up)


def solution(mesh):
    groups, members = mesh.devices.shape
    fine = Mesh(mesh.devices.reshape(groups, members // 2, 2), ("expert", *HEAD))
    placed = (
        P("expert", None),
        P("expert", None),
        P("expert", None),
        P("expert", None, HEAD),
        P("expert", HEAD, None),
        P(None, HEAD),
        P("expert", HEAD),
    )
    return jax.shard_map(
        per_device,
        mesh=fine,
        in_specs=placed,
        out_specs=(P("expert", HEAD), P("expert", None, HEAD)),
        check_vma=False,
    )
```

```python
import jax
import jax.numpy as jnp
from jax import lax
from jax.experimental import pallas as pl
from jax.experimental.pallas import tpu as pltpu
from jax.sharding import Mesh, PartitionSpec as P

F32 = jnp.float32
BF16 = jnp.bfloat16
HEAD = ("quarter", "parity", "core")
Z = HEAD[:2]
QUAD = 4
CHUNKS = 4
BACK_VMEM, SEND_VMEM, FORWARD_VMEM, WEIGHT_VMEM = 53, 53, 50, 50
MIB = 2**20
MOST = 4
ROWS = 2 * MOST
ANY = pl.BlockSpec(memory_space=pl.ANY)
VMEM = pl.BlockSpec(memory_space=pltpu.VMEM)
SMEM = pl.BlockSpec(memory_space=pltpu.SMEM)


def call(kernel, outs, *args, scalars=0, flops=0, in_hbm=(), out_hbm=(), scratch=(), vmem=32):
    single = not isinstance(outs, (list, tuple))
    moved = sum(a.size * a.dtype.itemsize for a in args)
    ins = [SMEM if i < scalars else ANY if i in in_hbm else VMEM for i in range(len(args))]
    places = [ANY if i in out_hbm else VMEM for i in range(1 if single else len(outs))]
    return pl.pallas_call(
        kernel,
        out_shape=outs,
        in_specs=ins,
        out_specs=places[0] if single else places,
        scratch_shapes=scratch,
        compiler_params=pltpu.CompilerParams(vmem_limit_bytes=vmem * MIB),
        cost_estimate=pl.CostEstimate(flops=flops, bytes_accessed=2 * moved, transcendentals=0),
    )(*args)


def shape(*dims, dtype=BF16):
    return jax.ShapeDtypeStruct(dims, dtype)


def dot(a, b, dims, precision=None):
    return lax.dot_general(a, b, (dims, ((), ())), precision=precision, preferred_element_type=F32)


def halves(me_ref, rows):
    half = rows.shape[1] // 2
    first = me_ref[0] % 2 == 0
    left, right = rows[:, :half], rows[:, half:]
    return jnp.where(first, left, right), jnp.where(first, right, left)


def joined(me_ref, own, other):
    first = me_ref[0] % 2 == 0
    own, other = own.astype(F32), other.astype(F32)
    return jnp.concatenate([jnp.where(first, own, other), jnp.where(first, other, own)], axis=1)


def back_kernel(me_ref, cot_hbm, out_w_hbm, keep_ref, give_ref, cot_ref, out_w_ref, sems):
    copies = [
        pltpu.make_async_copy(out_w_hbm, out_w_ref, sems.at[0]),
        pltpu.make_async_copy(cot_hbm, cot_ref, sems.at[1]),
    ]
    for copy in copies:
        copy.start()
    for copy in copies:
        copy.wait()
    part = dot(cot_ref[...], out_w_ref[...], ((1,), (1,)))
    keep, give = halves(me_ref, part)
    keep_ref[...] = keep
    give_ref[...] = give.astype(BF16)


def spread_kernel(keep_ref, got_ref, o_ref):
    rows = (keep_ref[...] + got_ref[...].astype(F32)).astype(BF16)
    for z in range(o_ref.shape[0]):
        o_ref[z] = rows


def sum_kernel(i_ref, o_ref):
    o_ref[...] = jnp.sum(i_ref[...].astype(F32), axis=0).astype(BF16)


def pick_kernel(me_ref, table_ref, coef_ref):
    count, tokens = coef_ref.shape
    top = table_ref.shape[0] // 2
    row = lax.broadcasted_iota(jnp.int32, (count, tokens), 0)
    expert = QUAD * (row // ROWS) + me_ref[0]
    score = jnp.zeros((count, tokens), jnp.int32)
    for k in range(top):
        q = table_ref[top + k : top + k + 1, :]
        score = score + jnp.where(table_ref[k : k + 1, :] == expert, q, 0)
    score = score.astype(F32)
    named = score > 0.0
    earlier = lax.broadcasted_iota(jnp.int32, (tokens, tokens), 0)
    later = lax.broadcasted_iota(jnp.int32, (tokens, tokens), 1)
    before = jnp.where(earlier < later, 1.0, 0.0).astype(BF16)
    rank = dot(jnp.where(named, 1.0, 0.0).astype(BF16), before, ((1,), (0,)))
    here = named & (rank == (row % MOST).astype(F32))
    coef_ref[...] = jnp.where(here, score, 0.0).astype(BF16)


def send_kernel(me_ref, table_ref, coef_ref, latent_ref, own_ref, other_ref, send_ref, buf, sems):
    count = send_ref.shape[0]
    top = table_ref.shape[0] // 2
    step = count // CHUNKS
    back = joined(me_ref, own_ref[...], other_ref[...]).astype(BF16)
    latent = latent_ref[...]
    total = jnp.sum(table_ref[top:, :].astype(F32), axis=0, keepdims=True)
    is_latent = lax.broadcasted_iota(jnp.int32, (step, 1), 0) % ROWS < MOST
    copies = []
    for i in range(CHUNKS):
        at = pl.ds(step * i, step)
        coef = coef_ref[at, :].astype(F32)
        gate = jnp.sum(coef / total, axis=1, keepdims=True)
        pick = jnp.where(coef > 0.0, 1.0, 0.0).astype(BF16)
        latent_rows = dot(pick, latent, ((1,), (0,)))
        back_rows = dot(pick, back, ((1,), (0,)))
        buf[at, :] = jnp.where(is_latent, latent_rows, gate * back_rows).astype(BF16)
        copies.append(pltpu.make_async_copy(buf.at[at, :], send_ref.at[at, :], sems.at[i]))
        copies[-1].start()
    for copy in copies:
        copy.wait()


def pack_kernel(me_ref, up_ref, down_ref, *outs):
    width, unit = up_ref.shape[1], up_ref.shape[2]
    for d, o_ref in enumerate(outs, 1):
        expert = me_ref[0] ^ d
        o_ref[0:width, :] = up_ref[expert]
        for b in range(width // unit):
            o_ref[width + unit * b : width + unit * (b + 1), :] = down_ref[
                expert, :, unit * b : unit * (b + 1)
            ]


class Copies:
    def __init__(self, sems):
        self.sems, self.used = sems, 0

    def start(self, source, target):
        copy = pltpu.make_async_copy(source, target, self.sems.at[self.used])
        self.used += 1
        copy.start()
        return copy

    def start_down(self, me, down_hbm, packs, down_ref):
        unit, width = down_hbm.shape[1:]
        started = [self.start(down_hbm.at[me], down_ref.at[0:unit, :])]
        for d, p in enumerate(packs, 1):
            at = pl.ds(unit * d, unit)
            for b in range(width // unit):
                block = p.at[pl.ds(width + unit * b, unit), :]
                started.append(self.start(block, down_ref.at[at, pl.ds(unit * b, unit)]))
        return started

    def start_up(self, me, up_hbm, packs, up_ref):
        width, unit = up_hbm.shape[1:]
        started = [self.start(up_hbm.at[me], up_ref.at[:, 0:unit])]
        for d, p in enumerate(packs, 1):
            started.append(self.start(p.at[pl.ds(0, width), :], up_ref.at[:, pl.ds(unit * d, unit)]))
        return started


def wait(copies):
    for copy in copies:
        copy.wait()


def latent_rows_of(count):
    return lax.broadcasted_iota(jnp.int32, (count, 1), 0) % ROWS < MOST


def forward_kernel(me_ref, rows_ref, up_hbm, down_hbm, *refs):
    packs, refs = refs[: QUAD - 1], refs[QUAD - 1 :]
    out_hbm, up_ref, down_ref, out_ref, sems = refs
    parts, count, strip = out_ref.shape
    copies = Copies(sems)
    ups = copies.start_up(me_ref[0], up_hbm, packs, up_ref)
    downs = copies.start_down(me_ref[0], down_hbm, packs, down_ref)
    is_latent = latent_rows_of(count)
    wait(ups)
    act = jnp.maximum(dot(rows_ref[...], up_ref[...], ((1,), (0,))), 0.0)
    hidden = act * act
    hidden = jnp.where(is_latent, hidden, pltpu.roll(hidden, MOST, 0)).astype(BF16)
    wait(downs)
    for q in range(parts):
        at = 2 * strip * q
        wide = dot(hidden, down_ref[:, at : at + 2 * strip], ((1,), (0,)))
        out_ref[q] = jnp.where(is_latent, wide[:, :strip], wide[:, strip:]).astype(BF16)
    wait([copies.start(out_ref, out_hbm)])


def weight_kernel(me_ref, rows_ref, up_hbm, down_hbm, *refs):
    packs, refs = refs[: QUAD - 1], refs[QUAD - 1 :]
    outs_hbm, refs = refs[:QUAD], refs[QUAD:]
    up_ref, down_ref, grad_ref, sems = refs
    unit = up_hbm.shape[2]
    count = rows_ref.shape[0]
    copies = Copies(sems)
    ups = copies.start_up(me_ref[0], up_hbm, packs, up_ref)
    downs = copies.start_down(me_ref[0], down_hbm, packs, down_ref)
    wait(ups)
    rows = rows_ref[...]
    act = jnp.maximum(dot(rows, up_ref[...], ((1,), (0,))), 0.0)
    wait(downs)
    hidden_grad = pltpu.roll(dot(rows, down_ref[...], ((1,), (1,))), count - MOST, 0)
    pre_grad = jnp.where(latent_rows_of(count), hidden_grad * 2.0 * act, 0.0).astype(BF16)
    grad_ref[...] = dot(rows, pre_grad, ((0,), (0,))).astype(BF16)
    wait([copies.start(grad_ref.at[:, pl.ds(unit * d, unit)], o) for d, o in enumerate(outs_hbm)])


def combine_kernel(rows_ref, coef_ref, gate_ref, o_ref):
    count = rows_ref.shape[0]
    is_left = lax.broadcasted_iota(jnp.int32, (count, 1), 0) % ROWS < MOST
    coef = coef_ref[...].astype(F32)
    left = jnp.where(is_left, coef, 0.0).astype(BF16)
    right = jnp.where(is_left, 0.0, coef).astype(BF16)
    rows = rows_ref[...]
    total = jnp.sum(gate_ref[...].astype(F32), axis=1, keepdims=True)
    parts = [dot(c, rows, ((0,), (0,))) / total for c in (left, right)]
    quarter = jnp.concatenate(parts, axis=1).astype(BF16)
    for member in range(o_ref.shape[0]):
        o_ref[member] = quarter


def mixed_kernel(parts_ref, out_w_ref, o_ref):
    members = parts_ref.shape[0]
    quarters = []
    for first in range(0, members, QUAD):
        quarters.append(jnp.sum(parts_ref[first : first + QUAD].astype(F32), axis=0))
    combined = jnp.concatenate(quarters, axis=1).astype(BF16)
    o_ref[...] = dot(combined, out_w_ref[...], ((1,), (0,))).astype(BF16)


def grad_kernel(me_ref, *refs):
    grads, o_ref = refs[:-1], refs[-1]
    for d, g_ref in enumerate(grads):
        o_ref[me_ref[0] ^ d] = g_ref[...]


def exchange(rows, axis):
    peers = lax.axis_size(axis)
    split = rows.reshape(peers, rows.shape[0] // peers, rows.shape[1])
    moved = lax.all_to_all(split, axis, split_axis=0, concat_axis=0, tiled=True)
    return moved.reshape(rows.shape)


def swap(array, distance, back=False):
    chips = lax.axis_size(Z)
    pairs = []
    for z in range(chips):
        for core in range(2):
            to = (z + 2 * core - 1) % chips if distance > 1 else z
            pairs.append((2 * z + core, 2 * to + core ^ (distance % 2)))
    return lax.ppermute(array, HEAD, [(b, a) for a, b in pairs] if back else pairs)


def sum_over_head(keep, give, beside=()):
    chips = lax.axis_size(Z)
    spread = call(spread_kernel, shape(chips, *keep.shape), keep, swap(give, 1))
    moved = lax.all_to_all(spread, Z, split_axis=0, concat_axis=0, tiled=True)
    moved, *beside = lax.optimization_barrier((moved, *beside))
    own = call(sum_kernel, shape(*keep.shape), moved)
    return own, swap(own, 1), *beside


def per_device(latent, routes, gate_q, up_weight, down_weight, out_weight, cotangent):
    groups = lax.axis_size("expert")
    tokens, width = latent.shape
    unit = up_weight.shape[2]
    count = groups * ROWS
    half = shape(tokens, width // 2)
    half_wide = shape(tokens, width // 2, dtype=F32)
    me = (2 * lax.axis_index("parity") + lax.axis_index("core")).astype(jnp.int32).reshape(1)
    table = jnp.concatenate([routes, gate_q], axis=1).T

    coef = call(pick_kernel, shape(count, tokens), me, table, scalars=1)
    packs = call(
        pack_kernel,
        [shape(2 * width, unit)] * (QUAD - 1),
        me, up_weight, down_weight, scalars=1,
    )
    packs = [swap(p, d) for d, p in enumerate(packs, 1)]

    back = call(
        back_kernel, [half_wide, half], me, cotangent, out_weight,
        scalars=1, flops=2 * tokens * width * cotangent.shape[1], in_hbm=(1, 2), vmem=BACK_VMEM,
        scratch=[
            pltpu.VMEM(cotangent.shape, BF16),
            pltpu.VMEM(out_weight.shape, BF16),
            pltpu.SemaphoreType.DMA((2,)),
        ],
    )
    *back, table, coef = sum_over_head(*back, beside=(table, coef))
    send = call(
        send_kernel,
        shape(count, width),
        me, table, coef, latent, *back,
        scalars=1, out_hbm=(0,), vmem=SEND_VMEM,
        scratch=[pltpu.VMEM((count, width), BF16), pltpu.SemaphoreType.DMA((CHUNKS,))],
    )
    rows = exchange(send, "expert")
    hidden = unit * QUAD
    copies = 2 * QUAD + 1 + (QUAD - 1) * (width // unit)
    up_space, down_space = pltpu.VMEM((width, hidden), BF16), pltpu.VMEM((hidden, width), BF16)
    parts = lax.axis_size("quarter")
    strip = width // parts // 2
    out = call(
        forward_kernel,
        shape(parts, count, strip),
        me, rows, up_weight, down_weight, *packs,
        scalars=1, flops=4 * count * width * hidden,
        in_hbm=range(2, 4 + QUAD), out_hbm=(0,), vmem=FORWARD_VMEM,
        scratch=[
            up_space, down_space,
            pltpu.VMEM((parts, count, strip), BF16), pltpu.SemaphoreType.DMA((copies,)),
        ],
    )
    grads = call(
        weight_kernel,
        [shape(width, unit)] * QUAD,
        me, rows, up_weight, down_weight, *packs,
        scalars=1, flops=6 * count * width * hidden,
        in_hbm=range(2, 4 + QUAD), out_hbm=range(QUAD), vmem=WEIGHT_VMEM,
        scratch=[up_space, down_space, up_space, pltpu.SemaphoreType.DMA((copies + QUAD,))],
    )
    moved = lax.all_to_all(out, "quarter", split_axis=0, concat_axis=0, tiled=True)
    moved, *grads = lax.optimization_barrier((moved, *grads))
    out = call(sum_kernel, shape(count, strip), moved)
    grads = [grads[0]] + [swap(g, d, back=True) for d, g in enumerate(grads[1:], 1)]
    returned, grads[2] = lax.optimization_barrier((exchange(out, "expert"), grads[2]))
    members = lax.axis_size(HEAD)
    comb = call(
        combine_kernel, shape(members, tokens, width // parts), returned, coef, gate_q
    )
    comb = lax.all_to_all(comb, HEAD, split_axis=0, concat_axis=0, tiled=True)
    mixed = call(
        mixed_kernel, shape(tokens, out_weight.shape[1]), comb, out_weight,
        flops=2 * tokens * width * out_weight.shape[1],
    )
    grad_up = call(grad_kernel, shape(*up_weight.shape), me, *grads, scalars=1)
    return (mixed, grad_up)


def solution(mesh):
    groups, members = mesh.devices.shape
    fine = Mesh(mesh.devices.reshape(groups, members // 4, 2, 2), ("expert", *HEAD))
    placed = (
        P("expert", None),
        P("expert", None),
        P("expert", None),
        P("expert", None, HEAD),
        P("expert", HEAD, None),
        P(None, HEAD),
        P("expert", HEAD),
    )
    return jax.shard_map(
        per_device,
        mesh=fine,
        in_specs=placed,
        out_specs=(P("expert", HEAD), P("expert", None, HEAD)),
        check_vma=False,
    )
```

```python
import jax
import jax.numpy as jnp
from jax import lax
from jax.experimental import pallas as pl
from jax.experimental.pallas import tpu as pltpu
from jax.sharding import Mesh, PartitionSpec as P

F32 = jnp.float32
BF16 = jnp.bfloat16
HEAD = ("z", "core")
QUAD = 4
CHUNKS = 4
BACK_VMEM, SEND_VMEM, FORWARD_VMEM, WEIGHT_VMEM = 53, 53, 50, 50
MIB = 2**20
MOST = 4
ROWS = 2 * MOST
ANY = pl.BlockSpec(memory_space=pl.ANY)
VMEM = pl.BlockSpec(memory_space=pltpu.VMEM)
SMEM = pl.BlockSpec(memory_space=pltpu.SMEM)


def call(kernel, outs, *args, scalars=0, flops=0, in_hbm=(), out_hbm=(), scratch=(), vmem=32):
    single = not isinstance(outs, (list, tuple))
    moved = sum(a.size * a.dtype.itemsize for a in args)
    ins = [SMEM if i < scalars else ANY if i in in_hbm else VMEM for i in range(len(args))]
    places = [ANY if i in out_hbm else VMEM for i in range(1 if single else len(outs))]
    return pl.pallas_call(
        kernel,
        out_shape=outs,
        in_specs=ins,
        out_specs=places[0] if single else places,
        scratch_shapes=scratch,
        compiler_params=pltpu.CompilerParams(vmem_limit_bytes=vmem * MIB),
        cost_estimate=pl.CostEstimate(flops=flops, bytes_accessed=2 * moved, transcendentals=0),
    )(*args)


def shape(*dims, dtype=BF16):
    return jax.ShapeDtypeStruct(dims, dtype)


def dot(a, b, dims, precision=None):
    return lax.dot_general(a, b, (dims, ((), ())), precision=precision, preferred_element_type=F32)


def halves(me_ref, rows):
    half = rows.shape[1] // 2
    first = me_ref[0] % 2 == 0
    left, right = rows[:, :half], rows[:, half:]
    return jnp.where(first, left, right), jnp.where(first, right, left)


def joined(me_ref, own, other):
    first = me_ref[0] % 2 == 0
    own, other = own.astype(F32), other.astype(F32)
    return jnp.concatenate([jnp.where(first, own, other), jnp.where(first, other, own)], axis=1)


def back_kernel(me_ref, cot_hbm, out_w_hbm, keep_ref, give_ref, cot_ref, out_w_ref, sems):
    copies = [
        pltpu.make_async_copy(out_w_hbm, out_w_ref, sems.at[0]),
        pltpu.make_async_copy(cot_hbm, cot_ref, sems.at[1]),
    ]
    for copy in copies:
        copy.start()
    for copy in copies:
        copy.wait()
    part = dot(cot_ref[...], out_w_ref[...], ((1,), (1,)))
    keep, give = halves(me_ref, part)
    keep_ref[...] = keep
    give_ref[...] = give.astype(BF16)


def spread_kernel(keep_ref, got_ref, o_ref):
    rows = (keep_ref[...] + got_ref[...].astype(F32)).astype(BF16)
    for z in range(o_ref.shape[0]):
        o_ref[z] = rows


def sum_kernel(i_ref, o_ref):
    o_ref[...] = jnp.sum(i_ref[...].astype(F32), axis=0).astype(BF16)


def pick_kernel(me_ref, table_ref, *coef_refs):
    count, tokens = coef_refs[0].shape
    top = table_ref.shape[0] // 2
    row = lax.broadcasted_iota(jnp.int32, (count, tokens), 0)
    earlier = lax.broadcasted_iota(jnp.int32, (tokens, tokens), 0)
    later = lax.broadcasted_iota(jnp.int32, (tokens, tokens), 1)
    before = jnp.where(earlier < later, 1.0, 0.0).astype(BF16)
    coefs = []
    for core in range(2):
        expert = QUAD * (row // ROWS) + (me_ref[0] - me_ref[0] % 2 + core)
        score = jnp.zeros((count, tokens), jnp.int32)
        for k in range(top):
            q = table_ref[top + k : top + k + 1, :]
            score = score + jnp.where(table_ref[k : k + 1, :] == expert, q, 0)
        score = score.astype(F32)
        named = score > 0.0
        rank = dot(jnp.where(named, 1.0, 0.0).astype(BF16), before, ((1,), (0,)))
        here = named & (rank == (row % MOST).astype(F32))
        coefs.append(jnp.where(here, score, 0.0))
    first = me_ref[0] % 2 == 0
    for ref, coef in zip(coef_refs, [jnp.where(first, *coefs), *coefs]):
        ref[...] = coef.astype(BF16)


def send_kernel(table_ref, coef_ref, coef0_ref, coef1_ref, latent_ref, half_ref, send_ref, buf, sems):
    count, width = send_ref.shape
    half = width // 2
    top = table_ref.shape[0] // 2
    step = count // CHUNKS
    back = half_ref[...]
    latent = latent_ref[...]
    total = jnp.sum(table_ref[top:, :].astype(F32), axis=0, keepdims=True)
    is_latent = lax.broadcasted_iota(jnp.int32, (step, 1), 0) % ROWS < MOST
    copies = []
    for i in range(CHUNKS):
        at = pl.ds(step * i, step)
        pick = jnp.where(coef_ref[at, :].astype(F32) > 0.0, 1.0, 0.0).astype(BF16)
        latent_rows = dot(pick, latent, ((1,), (0,)))
        for core, ref in enumerate((coef0_ref, coef1_ref)):
            coef = ref[at, :].astype(F32)
            gate = jnp.sum(coef / total, axis=1, keepdims=True)
            pick = jnp.where(coef > 0.0, 1.0, 0.0).astype(BF16)
            rows = gate * dot(pick, back, ((1,), (0,)))
            columns = slice(half * core, half * core + half)
            buf[at, columns] = jnp.where(is_latent, latent_rows[:, columns], rows).astype(BF16)
        copies.append(pltpu.make_async_copy(buf.at[at, :], send_ref.at[at, :], sems.at[i]))
        copies[-1].start()
    for copy in copies:
        copy.wait()


def other_kernel(me_ref, rows_ref, o_ref):
    half = o_ref.shape[1]
    first = me_ref[0] % 2 == 0
    o_ref[...] = jnp.where(first, rows_ref[:, half:], rows_ref[:, :half])


def pack_kernel(me_ref, up_ref, down_ref, *outs):
    width, unit = up_ref.shape[1], up_ref.shape[2]
    for d, o_ref in enumerate(outs, 1):
        expert = me_ref[0] ^ d
        o_ref[0:width, :] = up_ref[expert]
        for b in range(width // unit):
            o_ref[width + unit * b : width + unit * (b + 1), :] = down_ref[
                expert, :, unit * b : unit * (b + 1)
            ]


class Copies:
    def __init__(self, sems):
        self.sems, self.used = sems, 0

    def start(self, source, target):
        copy = pltpu.make_async_copy(source, target, self.sems.at[self.used])
        self.used += 1
        copy.start()
        return copy

    def start_down(self, me, down_hbm, packs, down_ref):
        unit, width = down_hbm.shape[1:]
        started = [self.start(down_hbm.at[me], down_ref.at[0:unit, :])]
        for d, p in enumerate(packs, 1):
            at = pl.ds(unit * d, unit)
            for b in range(width // unit):
                block = p.at[pl.ds(width + unit * b, unit), :]
                started.append(self.start(block, down_ref.at[at, pl.ds(unit * b, unit)]))
        return started

    def start_up(self, me, up_hbm, packs, up_ref):
        width, unit = up_hbm.shape[1:]
        started = [self.start(up_hbm.at[me], up_ref.at[:, 0:unit])]
        for d, p in enumerate(packs, 1):
            started.append(self.start(p.at[pl.ds(0, width), :], up_ref.at[:, pl.ds(unit * d, unit)]))
        return started


def wait(copies):
    for copy in copies:
        copy.wait()


def latent_rows_of(count):
    return lax.broadcasted_iota(jnp.int32, (count, 1), 0) % ROWS < MOST


def forward_kernel(me_ref, rows_ref, up_hbm, down_hbm, *refs):
    packs, refs = refs[: QUAD - 1], refs[QUAD - 1 :]
    out_hbm, up_ref, down_ref, out_ref, sems = refs
    count, half = out_ref.shape
    copies = Copies(sems)
    ups = copies.start_up(me_ref[0], up_hbm, packs, up_ref)
    downs = copies.start_down(me_ref[0], down_hbm, packs, down_ref)
    is_latent = latent_rows_of(count)
    wait(ups)
    act = jnp.maximum(dot(rows_ref[...], up_ref[...], ((1,), (0,))), 0.0)
    hidden = act * act
    hidden = jnp.where(is_latent, hidden, pltpu.roll(hidden, MOST, 0)).astype(BF16)
    wait(downs)
    left = dot(hidden, down_ref[:, :half], ((1,), (0,)))
    right = dot(hidden, down_ref[:, half:], ((1,), (0,)))
    out_ref[...] = jnp.where(is_latent, left, right).astype(BF16)
    wait([copies.start(out_ref, out_hbm)])


def weight_kernel(me_ref, rows_ref, got_ref, up_hbm, down_hbm, *refs):
    packs, refs = refs[: QUAD - 1], refs[QUAD - 1 :]
    outs_hbm, refs = refs[:QUAD], refs[QUAD:]
    up_ref, down_ref, grad_ref, sems = refs
    unit = up_hbm.shape[2]
    count = rows_ref.shape[0]
    copies = Copies(sems)
    ups = copies.start_up(me_ref[0], up_hbm, packs, up_ref)
    downs = copies.start_down(me_ref[0], down_hbm, packs, down_ref)
    wait(ups)
    rows = rows_ref[...]
    act = jnp.maximum(dot(rows, up_ref[...], ((1,), (0,))), 0.0)
    wait(downs)
    half = got_ref.shape[1]
    first = me_ref[0] % 2 == 0
    own, got = jnp.where(first, rows[:, :half], rows[:, half:]), got_ref[...]
    grads = (jnp.where(first, own, got), jnp.where(first, got, own))
    hidden_grad = dot(grads[0], down_ref[:, :half], ((1,), (1,)))
    hidden_grad = hidden_grad + dot(grads[1], down_ref[:, half:], ((1,), (1,)))
    hidden_grad = pltpu.roll(hidden_grad, count - MOST, 0)
    pre_grad = jnp.where(latent_rows_of(count), hidden_grad * 2.0 * act, 0.0).astype(BF16)
    grad_ref[...] = dot(rows, pre_grad, ((0,), (0,))).astype(BF16)
    wait([copies.start(grad_ref.at[:, pl.ds(unit * d, unit)], o) for d, o in enumerate(outs_hbm)])


def combine_kernel(me_ref, rows_ref, coef_ref, gate_ref, keep_ref, give_ref):
    count = rows_ref.shape[0]
    is_left = lax.broadcasted_iota(jnp.int32, (count, 1), 0) % ROWS < MOST
    coef = coef_ref[...].astype(F32)
    left = jnp.where(is_left, coef, 0.0).astype(BF16)
    right = jnp.where(is_left, 0.0, coef).astype(BF16)
    rows = rows_ref[...]
    total = jnp.sum(gate_ref[...].astype(F32), axis=1, keepdims=True)
    parts = [dot(c, rows, ((0,), (0,))) / total for c in (left, right)]
    keep, give = halves(me_ref, jnp.concatenate(parts, axis=1))
    keep_ref[...] = keep
    give_ref[...] = give.astype(BF16)


def mixed_kernel(me_ref, own_ref, other_ref, out_w_ref, o_ref):
    combined = joined(me_ref, own_ref[...], other_ref[...]).astype(BF16)
    o_ref[...] = dot(combined, out_w_ref[...], ((1,), (0,))).astype(BF16)


def grad_kernel(me_ref, *refs):
    grads, o_ref = refs[:-1], refs[-1]
    for d, g_ref in enumerate(grads):
        o_ref[me_ref[0] ^ d] = g_ref[...]


def exchange(rows, axis):
    peers = lax.axis_size(axis)
    split = rows.reshape(peers, rows.shape[0] // peers, rows.shape[1])
    moved = lax.all_to_all(split, axis, split_axis=0, concat_axis=0, tiled=True)
    return moved.reshape(rows.shape)


def swap(array, distance, back=False):
    chips = lax.axis_size("z")
    pairs = []
    for z in range(chips):
        for core in range(2):
            to = (z + 2 * core - 1) % chips if distance > 1 else z
            pairs.append((2 * z + core, 2 * to + core ^ (distance % 2)))
    return lax.ppermute(array, HEAD, [(b, a) for a, b in pairs] if back else pairs)


def sum_over_head(keep, give, beside=()):
    chips = lax.axis_size("z")
    spread = call(spread_kernel, shape(chips, *keep.shape), keep, swap(give, 1))
    moved = lax.all_to_all(spread, "z", split_axis=0, concat_axis=0, tiled=True)
    moved, *beside = lax.optimization_barrier((moved, *beside))
    return call(sum_kernel, shape(*keep.shape), moved), *beside


def per_device(latent, routes, gate_q, up_weight, down_weight, out_weight, cotangent):
    groups = lax.axis_size("expert")
    tokens, width = latent.shape
    unit = up_weight.shape[2]
    count = groups * ROWS
    half = shape(tokens, width // 2)
    half_wide = shape(tokens, width // 2, dtype=F32)
    me = (2 * (lax.axis_index("z") & 1) + lax.axis_index("core")).astype(jnp.int32).reshape(1)
    table = jnp.concatenate([routes, gate_q], axis=1).T

    coefs = call(pick_kernel, [shape(count, tokens)] * 3, me, table, scalars=1)
    packs = call(
        pack_kernel,
        [shape(2 * width, unit)] * (QUAD - 1),
        me, up_weight, down_weight, scalars=1,
    )
    packs = [swap(p, d) for d, p in enumerate(packs, 1)]

    back = call(
        back_kernel, [half_wide, half], me, cotangent, out_weight,
        scalars=1, flops=2 * tokens * width * cotangent.shape[1], in_hbm=(1, 2), vmem=BACK_VMEM,
        scratch=[
            pltpu.VMEM(cotangent.shape, BF16),
            pltpu.VMEM(out_weight.shape, BF16),
            pltpu.SemaphoreType.DMA((2,)),
        ],
    )
    back, table, *coefs = sum_over_head(*back, beside=(table, *coefs))
    send = call(
        send_kernel,
        shape(count, width),
        table, *coefs, latent, back,
        out_hbm=(0,), vmem=SEND_VMEM,
        scratch=[pltpu.VMEM((count, width), BF16), pltpu.SemaphoreType.DMA((CHUNKS,))],
    )
    rows = exchange(send, "expert")
    hidden = unit * QUAD
    copies = 2 * QUAD + 1 + (QUAD - 1) * (width // unit)
    up_space, down_space = pltpu.VMEM((width, hidden), BF16), pltpu.VMEM((hidden, width), BF16)
    out = call(
        forward_kernel,
        shape(count, width // 2),
        me, rows, up_weight, down_weight, *packs,
        scalars=1, flops=4 * count * width * hidden,
        in_hbm=range(2, 4 + QUAD), out_hbm=(0,), vmem=FORWARD_VMEM,
        scratch=[
            up_space, down_space,
            pltpu.VMEM((count, width // 2), BF16), pltpu.SemaphoreType.DMA((copies,)),
        ],
    )
    rows, out = lax.optimization_barrier((rows, out))
    got = swap(call(other_kernel, shape(count, width // 2), me, rows, scalars=1), 1)
    grads = call(
        weight_kernel,
        [shape(width, unit)] * QUAD,
        me, rows, got, up_weight, down_weight, *packs,
        scalars=1, flops=6 * count * width * hidden,
        in_hbm=range(3, 5 + QUAD), out_hbm=range(QUAD), vmem=WEIGHT_VMEM,
        scratch=[up_space, down_space, up_space, pltpu.SemaphoreType.DMA((copies + QUAD,))],
    )
    grads = [grads[0]] + [swap(g, d, back=True) for d, g in enumerate(grads[1:], 1)]
    returned, *grads[1:3] = lax.optimization_barrier((exchange(out, "expert"), *grads[1:3]))
    grad_up = call(grad_kernel, shape(*up_weight.shape), me, *grads, scalars=1)
    comb = call(combine_kernel, [half_wide, half], me, returned, coefs[0], gate_q, scalars=1)
    (comb,) = sum_over_head(*comb)
    mixed = call(
        mixed_kernel, shape(tokens, out_weight.shape[1]), me, comb, swap(comb, 1), out_weight,
        scalars=1, flops=2 * tokens * width * out_weight.shape[1],
    )
    return (mixed, grad_up)


def solution(mesh):
    groups, members = mesh.devices.shape
    fine = Mesh(mesh.devices.reshape(groups, members // 2, 2), ("expert", *HEAD))
    placed = (
        P("expert", None),
        P("expert", None),
        P("expert", None),
        P("expert", None, HEAD),
        P("expert", HEAD, None),
        P(None, HEAD),
        P("expert", HEAD),
    )
    return jax.shard_map(
        per_device,
        mesh=fine,
        in_specs=placed,
        out_specs=(P("expert", HEAD), P("expert", None, HEAD)),
        check_vma=False,
    )
```

```python
import jax
import jax.numpy as jnp
from jax import lax
from jax.experimental import pallas as pl
from jax.experimental.pallas import tpu as pltpu
from jax.sharding import Mesh, PartitionSpec as P

F32 = jnp.float32
BF16 = jnp.bfloat16
HEAD = ("z", "core")
QUAD = 4
CHUNKS = 4
BACK_VMEM, SEND_VMEM, FORWARD_VMEM, WEIGHT_VMEM = 53, 53, 50, 50
MIB = 2**20
MOST = 4
ROWS = 2 * MOST
ANY = pl.BlockSpec(memory_space=pl.ANY)
VMEM = pl.BlockSpec(memory_space=pltpu.VMEM)
SMEM = pl.BlockSpec(memory_space=pltpu.SMEM)


def call(kernel, outs, *args, scalars=0, flops=0, in_hbm=(), out_hbm=(), scratch=(), vmem=32):
    single = not isinstance(outs, (list, tuple))
    moved = sum(a.size * a.dtype.itemsize for a in args)
    ins = [SMEM if i < scalars else ANY if i in in_hbm else VMEM for i in range(len(args))]
    places = [ANY if i in out_hbm else VMEM for i in range(1 if single else len(outs))]
    return pl.pallas_call(
        kernel,
        out_shape=outs,
        in_specs=ins,
        out_specs=places[0] if single else places,
        scratch_shapes=scratch,
        compiler_params=pltpu.CompilerParams(vmem_limit_bytes=vmem * MIB),
        cost_estimate=pl.CostEstimate(flops=flops, bytes_accessed=2 * moved, transcendentals=0),
    )(*args)


def shape(*dims, dtype=BF16):
    return jax.ShapeDtypeStruct(dims, dtype)


def dot(a, b, dims, precision=None):
    return lax.dot_general(a, b, (dims, ((), ())), precision=precision, preferred_element_type=F32)


def halves(me_ref, rows):
    half = rows.shape[1] // 2
    first = me_ref[0] % 2 == 0
    left, right = rows[:, :half], rows[:, half:]
    return jnp.where(first, left, right), jnp.where(first, right, left)


def joined(me_ref, own, other):
    first = me_ref[0] % 2 == 0
    own, other = own.astype(F32), other.astype(F32)
    return jnp.concatenate([jnp.where(first, own, other), jnp.where(first, other, own)], axis=1)


def back_kernel(me_ref, cot_hbm, out_w_hbm, keep_ref, give_ref, cot_ref, out_w_ref, sems):
    copies = [
        pltpu.make_async_copy(out_w_hbm, out_w_ref, sems.at[0]),
        pltpu.make_async_copy(cot_hbm, cot_ref, sems.at[1]),
    ]
    for copy in copies:
        copy.start()
    for copy in copies:
        copy.wait()
    part = dot(cot_ref[...], out_w_ref[...], ((1,), (1,)))
    keep, give = halves(me_ref, part)
    keep_ref[...] = keep
    give_ref[...] = give.astype(BF16)


def spread_kernel(keep_ref, got_ref, o_ref):
    rows = (keep_ref[...] + got_ref[...].astype(F32)).astype(BF16)
    for z in range(o_ref.shape[0]):
        o_ref[z] = rows


def sum_kernel(i_ref, o_ref):
    o_ref[...] = jnp.sum(i_ref[...].astype(F32), axis=0).astype(BF16)


def pick_kernel(me_ref, table_ref, latent_ref, kept_ref, *coef_refs):
    kept_ref[...] = latent_ref[...]
    count, tokens = coef_refs[0].shape
    top = table_ref.shape[0] // 2
    row = lax.broadcasted_iota(jnp.int32, (count, tokens), 0)
    earlier = lax.broadcasted_iota(jnp.int32, (tokens, tokens), 0)
    later = lax.broadcasted_iota(jnp.int32, (tokens, tokens), 1)
    before = jnp.where(earlier < later, 1.0, 0.0).astype(BF16)
    coefs = []
    for core in range(2):
        expert = QUAD * (row // ROWS) + (me_ref[0] - me_ref[0] % 2 + core)
        score = jnp.zeros((count, tokens), jnp.int32)
        for k in range(top):
            q = table_ref[top + k : top + k + 1, :]
            score = score + jnp.where(table_ref[k : k + 1, :] == expert, q, 0)
        score = score.astype(F32)
        named = score > 0.0
        rank = dot(jnp.where(named, 1.0, 0.0).astype(BF16), before, ((1,), (0,)))
        here = named & (rank == (row % MOST).astype(F32))
        coefs.append(jnp.where(here, score, 0.0))
    first = me_ref[0] % 2 == 0
    for ref, coef in zip(coef_refs, [jnp.where(first, *coefs), *coefs]):
        ref[...] = coef.astype(BF16)


def send_kernel(table_ref, coef_ref, coef0_ref, coef1_ref, latent_ref, half_ref, send_ref, buf, sems):
    count, width = send_ref.shape
    half = width // 2
    top = table_ref.shape[0] // 2
    step = count // CHUNKS
    back = half_ref[...]
    latent = latent_ref[...]
    total = jnp.sum(table_ref[top:, :].astype(F32), axis=0, keepdims=True)
    is_latent = lax.broadcasted_iota(jnp.int32, (step, 1), 0) % ROWS < MOST
    copies = []
    for i in range(CHUNKS):
        at = pl.ds(step * i, step)
        pick = jnp.where(coef_ref[at, :].astype(F32) > 0.0, 1.0, 0.0).astype(BF16)
        latent_rows = dot(pick, latent, ((1,), (0,)))
        for core, ref in enumerate((coef0_ref, coef1_ref)):
            coef = ref[at, :].astype(F32)
            gate = jnp.sum(coef / total, axis=1, keepdims=True)
            pick = jnp.where(coef > 0.0, 1.0, 0.0).astype(BF16)
            rows = gate * dot(pick, back, ((1,), (0,)))
            columns = slice(half * core, half * core + half)
            buf[at, columns] = jnp.where(is_latent, latent_rows[:, columns], rows).astype(BF16)
        copies.append(pltpu.make_async_copy(buf.at[at, :], send_ref.at[at, :], sems.at[i]))
        copies[-1].start()
    for copy in copies:
        copy.wait()


def other_kernel(me_ref, rows_ref, o_ref):
    half = o_ref.shape[1]
    first = me_ref[0] % 2 == 0
    o_ref[...] = jnp.where(first, rows_ref[:, half:], rows_ref[:, :half])


def pack_kernel(me_ref, up_ref, down_ref, *outs):
    width, unit = up_ref.shape[1], up_ref.shape[2]
    for d, o_ref in enumerate(outs, 1):
        expert = me_ref[0] ^ d
        o_ref[0:width, :] = up_ref[expert]
        for b in range(width // unit):
            o_ref[width + unit * b : width + unit * (b + 1), :] = down_ref[
                expert, :, unit * b : unit * (b + 1)
            ]


class Copies:
    def __init__(self, sems):
        self.sems, self.used = sems, 0

    def start(self, source, target):
        copy = pltpu.make_async_copy(source, target, self.sems.at[self.used])
        self.used += 1
        copy.start()
        return copy

    def start_down(self, me, down_hbm, packs, down_ref):
        unit, width = down_hbm.shape[1:]
        started = [self.start(down_hbm.at[me], down_ref.at[0:unit, :])]
        for d, p in enumerate(packs, 1):
            at = pl.ds(unit * d, unit)
            for b in range(width // unit):
                block = p.at[pl.ds(width + unit * b, unit), :]
                started.append(self.start(block, down_ref.at[at, pl.ds(unit * b, unit)]))
        return started

    def start_up(self, me, up_hbm, packs, up_ref):
        width, unit = up_hbm.shape[1:]
        started = [self.start(up_hbm.at[me], up_ref.at[:, 0:unit])]
        for d, p in enumerate(packs, 1):
            started.append(self.start(p.at[pl.ds(0, width), :], up_ref.at[:, pl.ds(unit * d, unit)]))
        return started


def wait(copies):
    for copy in copies:
        copy.wait()


def latent_rows_of(count):
    return lax.broadcasted_iota(jnp.int32, (count, 1), 0) % ROWS < MOST


def forward_kernel(me_ref, rows_ref, up_hbm, down_hbm, *refs):
    packs, refs = refs[: QUAD - 1], refs[QUAD - 1 :]
    out_hbm, up_ref, down_ref, out_ref, sems = refs
    count, half = out_ref.shape
    copies = Copies(sems)
    ups = copies.start_up(me_ref[0], up_hbm, packs, up_ref)
    downs = copies.start_down(me_ref[0], down_hbm, packs, down_ref)
    is_latent = latent_rows_of(count)
    wait(ups)
    act = jnp.maximum(dot(rows_ref[...], up_ref[...], ((1,), (0,))), 0.0)
    hidden = act * act
    hidden = jnp.where(is_latent, hidden, pltpu.roll(hidden, MOST, 0)).astype(BF16)
    wait(downs)
    left = dot(hidden, down_ref[:, :half], ((1,), (0,)))
    right = dot(hidden, down_ref[:, half:], ((1,), (0,)))
    out_ref[...] = jnp.where(is_latent, left, right).astype(BF16)
    wait([copies.start(out_ref, out_hbm)])


def weight_kernel(me_ref, rows_ref, got_ref, up_hbm, down_hbm, *refs):
    packs, refs = refs[: QUAD - 1], refs[QUAD - 1 :]
    outs_hbm, refs = refs[:QUAD], refs[QUAD:]
    up_ref, down_ref, grad_ref, sems = refs
    unit = up_hbm.shape[2]
    count = rows_ref.shape[0]
    copies = Copies(sems)
    ups = copies.start_up(me_ref[0], up_hbm, packs, up_ref)
    downs = copies.start_down(me_ref[0], down_hbm, packs, down_ref)
    wait(ups)
    rows = rows_ref[...]
    act = jnp.maximum(dot(rows, up_ref[...], ((1,), (0,))), 0.0)
    wait(downs)
    half = got_ref.shape[1]
    first = me_ref[0] % 2 == 0
    own, got = jnp.where(first, rows[:, :half], rows[:, half:]), got_ref[...]
    grads = (jnp.where(first, own, got), jnp.where(first, got, own))
    hidden_grad = dot(grads[0], down_ref[:, :half], ((1,), (1,)))
    hidden_grad = hidden_grad + dot(grads[1], down_ref[:, half:], ((1,), (1,)))
    hidden_grad = pltpu.roll(hidden_grad, count - MOST, 0)
    pre_grad = jnp.where(latent_rows_of(count), hidden_grad * 2.0 * act, 0.0).astype(BF16)
    grad_ref[...] = dot(rows, pre_grad, ((0,), (0,))).astype(BF16)
    wait([copies.start(grad_ref.at[:, pl.ds(unit * d, unit)], o) for d, o in enumerate(outs_hbm)])


def combine_kernel(me_ref, rows_ref, coef_ref, gate_ref, keep_ref, give_ref):
    count = rows_ref.shape[0]
    is_left = lax.broadcasted_iota(jnp.int32, (count, 1), 0) % ROWS < MOST
    coef = coef_ref[...].astype(F32)
    left = jnp.where(is_left, coef, 0.0).astype(BF16)
    right = jnp.where(is_left, 0.0, coef).astype(BF16)
    rows = rows_ref[...]
    total = jnp.sum(gate_ref[...].astype(F32), axis=1, keepdims=True)
    parts = [dot(c, rows, ((0,), (0,))) / total for c in (left, right)]
    keep, give = halves(me_ref, jnp.concatenate(parts, axis=1))
    keep_ref[...] = keep
    give_ref[...] = give.astype(BF16)


def mixed_kernel(me_ref, own_ref, other_ref, out_w_ref, o_ref):
    combined = joined(me_ref, own_ref[...], other_ref[...]).astype(BF16)
    o_ref[...] = dot(combined, out_w_ref[...], ((1,), (0,))).astype(BF16)


def grad_kernel(me_ref, *refs):
    grads, o_ref = refs[:-1], refs[-1]
    for d, g_ref in enumerate(grads):
        o_ref[me_ref[0] ^ d] = g_ref[...]


def exchange(rows, axis):
    peers = lax.axis_size(axis)
    split = rows.reshape(peers, rows.shape[0] // peers, rows.shape[1])
    moved = lax.all_to_all(split, axis, split_axis=0, concat_axis=0, tiled=True)
    return moved.reshape(rows.shape)


def swap(array, distance, back=False):
    chips = lax.axis_size("z")
    pairs = []
    for z in range(chips):
        for core in range(2):
            to = (z + 2 * core - 1) % chips if distance > 1 else z
            pairs.append((2 * z + core, 2 * to + core ^ (distance % 2)))
    return lax.ppermute(array, HEAD, [(b, a) for a, b in pairs] if back else pairs)


def sum_over_head(keep, give, beside=(), before=()):
    chips = lax.axis_size("z")
    got, *before = lax.optimization_barrier((swap(give, 1), *before))
    spread = call(spread_kernel, shape(chips, *keep.shape), keep, got)
    moved = lax.all_to_all(spread, "z", split_axis=0, concat_axis=0, tiled=True)
    moved, *beside = lax.optimization_barrier((moved, *beside))
    return call(sum_kernel, shape(*keep.shape), moved), *beside, *before


def per_device(latent, routes, gate_q, up_weight, down_weight, out_weight, cotangent):
    groups = lax.axis_size("expert")
    tokens, width = latent.shape
    unit = up_weight.shape[2]
    count = groups * ROWS
    half = shape(tokens, width // 2)
    half_wide = shape(tokens, width // 2, dtype=F32)
    me = (2 * (lax.axis_index("z") & 1) + lax.axis_index("core")).astype(jnp.int32).reshape(1)
    table = jnp.concatenate([routes, gate_q], axis=1).T

    latent, *coefs = call(
        pick_kernel, [shape(tokens, width)] + [shape(count, tokens)] * 3, me, table, latent, scalars=1
    )
    packs = call(
        pack_kernel,
        [shape(2 * width, unit)] * (QUAD - 1),
        me, up_weight, down_weight, scalars=1,
    )
    packs = [swap(p, d) for d, p in enumerate(packs, 1)]

    back = call(
        back_kernel, [half_wide, half], me, cotangent, out_weight,
        scalars=1, flops=2 * tokens * width * cotangent.shape[1], in_hbm=(1, 2), vmem=BACK_VMEM,
        scratch=[
            pltpu.VMEM(cotangent.shape, BF16),
            pltpu.VMEM(out_weight.shape, BF16),
            pltpu.SemaphoreType.DMA((2,)),
        ],
    )
    back, table, latent, *coefs = sum_over_head(*back, beside=(table, latent, *coefs))
    send = call(
        send_kernel,
        shape(count, width),
        table, *coefs, latent, back,
        out_hbm=(0,), vmem=SEND_VMEM,
        scratch=[pltpu.VMEM((count, width), BF16), pltpu.SemaphoreType.DMA((CHUNKS,))],
    )
    rows = exchange(send, "expert")
    hidden = unit * QUAD
    copies = 2 * QUAD + 1 + (QUAD - 1) * (width // unit)
    up_space, down_space = pltpu.VMEM((width, hidden), BF16), pltpu.VMEM((hidden, width), BF16)
    out = call(
        forward_kernel,
        shape(count, width // 2),
        me, rows, up_weight, down_weight, *packs,
        scalars=1, flops=4 * count * width * hidden,
        in_hbm=range(2, 4 + QUAD), out_hbm=(0,), vmem=FORWARD_VMEM,
        scratch=[
            up_space, down_space,
            pltpu.VMEM((count, width // 2), BF16), pltpu.SemaphoreType.DMA((copies,)),
        ],
    )
    rows, out = lax.optimization_barrier((rows, out))
    got = swap(call(other_kernel, shape(count, width // 2), me, rows, scalars=1), 1)
    grads = call(
        weight_kernel,
        [shape(width, unit)] * QUAD,
        me, rows, got, up_weight, down_weight, *packs,
        scalars=1, flops=6 * count * width * hidden,
        in_hbm=range(3, 5 + QUAD), out_hbm=range(QUAD), vmem=WEIGHT_VMEM,
        scratch=[up_space, down_space, up_space, pltpu.SemaphoreType.DMA((copies + QUAD,))],
    )
    grads = [grads[0]] + [swap(g, d, back=True) for d, g in enumerate(grads[1:], 1)]
    returned, grads[1] = lax.optimization_barrier((exchange(out, "expert"), grads[1]))
    comb = call(combine_kernel, [half_wide, half], me, returned, coefs[0], gate_q, scalars=1)
    comb, grads[2] = sum_over_head(*comb, before=(grads[2],))
    mixed = call(
        mixed_kernel, shape(tokens, out_weight.shape[1]), me, comb, swap(comb, 1), out_weight,
        scalars=1, flops=2 * tokens * width * out_weight.shape[1],
    )
    grad_up = call(grad_kernel, shape(*up_weight.shape), me, *grads, scalars=1)
    return (mixed, grad_up)


def solution(mesh):
    groups, members = mesh.devices.shape
    fine = Mesh(mesh.devices.reshape(groups, members // 2, 2), ("expert", *HEAD))
    placed = (
        P("expert", None),
        P("expert", None),
        P("expert", None),
        P("expert", None, HEAD),
        P("expert", HEAD, None),
        P(None, HEAD),
        P("expert", HEAD),
    )
    return jax.shard_map(
        per_device,
        mesh=fine,
        in_specs=placed,
        out_specs=(P("expert", HEAD), P("expert", None, HEAD)),
        check_vma=False,
    )
```
